32 devices in a mesh: grp: 2 (over y), dp: 4 (over x, core), mp: 4 (over z).
Axes of the slice: x: 2, y: 2, z: 4, core: 2. Of those that a mesh axis runs over, the one named last changes fastest.
Arguments:
- teacher_hidden: bfloat16 [4096, 8192], P('dp', 'mp'), may hold values from -6 to 6
- teacher_gain: bfloat16 [8192], P('mp'), may hold values from 0.25 to 1.75
- teacher_value: bfloat16 [8192, 1024], P('mp', 'grp'), may hold values from -0.0625 to 0.0625
- student_hidden: bfloat16 [4096, 4096], P(('dp', 'mp')), may hold values from -6 to 6
- student_gain: bfloat16 [4096], replicated, may hold values from 0.25 to 1.75
- student_value: bfloat16 [4096, 1024], P(('dp', 'mp'), 'grp'), may hold values from -0.09375 to 0.09375
- segment_ids: int32 [4, 1024], P('dp'), may hold values from 0 to 7, never falling along the last dimension, each value on 1 to 384 neighbouring positions
Outputs:
- value_grad: float32 [4096, 1024], P(('dp', 'mp'), 'grp')
The draws below stay inside these ranges and needn't reach their ends.
Inputs may be any that keep to these rules, and one draw needn't show every extreme that they name: `segment_ids`: in every row the ids never fall; each id from 0 to 7 covers 1 to 384 consecutive positions, and one covers exactly 384.
All inputs are finite; a program needn't handle non-finite values.
Results may differ from the reference program's by a relative error of at most 0.0031.
Values may be sent and summed in bfloat16 or wider, within the bound.
No kernel may reach another device: no remote copies, remote signals or barrier semaphores. Data moves between devices by JAX's collectives and lax.ppermute only.
A program may use at most 64 MiB of HBM per device.

```python
import math
import jax
import jax.numpy as jnp
import numpy as np
from jax import lax

DT = 8192
DS = 4096
KV = 1024
LEN = 1024
NSEG = 8
MOST = 384
TOKENS = 4096
ROWS = 4


def raised(array, own_key, source, target, blocks, factor):
    def block_of(dim):
        return (jnp.arange(array.shape[dim]) // (array.shape[dim] // blocks)).reshape((-1,) + (1,) * (array.ndim - 1 - dim))

    near = jax.random.permutation(own_key, blocks)[block_of(target)]
    other_side = (block_of(target) + blocks // 2) % blocks
    return jnp.where((block_of(source) == near) | (block_of(source) == other_side), factor * array, array)


def block_scale(stream_key, dims, cuts, least, largest):
    gain, own = 1.0, jax.random.fold_in(stream_key, 6)
    for dim, blocks in cuts:
        steps = jnp.exp(jax.random.uniform(jax.random.fold_in(own, dim), (blocks,), jnp.float32, least / len(cuts), largest / len(cuts)))
        gain = gain * jnp.repeat(steps, dims[dim] // blocks).reshape([-1 if axis == dim else 1 for axis in range(len(dims))])
    return gain


def length_profile(count, total, limit, slope):
    loads = [(1 << 20) // math.isqrt(grade ** slope) + 1 for grade in range(2, count + 1)]
    surplus, given = total - limit - (count - 1), [1] * (count - 1)
    while surplus > 0:
        movable = [i for i in range(count - 1) if given[i] < limit]
        whole, budget = sum([loads[i] for i in movable]), surplus
        for i in movable:
            addition = min(limit - given[i], max(1, budget * loads[i] // whole), surplus)
            given[i] = given[i] + addition
            surplus = surplus - addition
    return np.array([limit] + given)


def ragged_sizes(stream_key, number_of, total, reach, skew):
    if number_of == 2:
        one = jax.random.randint(stream_key, (), max(1, total - reach), min(reach, total - 1) + 1)
        return jnp.stack([one, total - one])
    lengths = jnp.asarray(length_profile(number_of, total, reach, skew), jnp.int32)
    twos = (number_of - 1) // 2
    source_of, sink = lengths[1:1 + 2 * twos:2], lengths[2:2 + 2 * twos:2]
    margin = jnp.minimum(source_of - 1, reach - sink)
    passed = jax.random.randint(jax.random.fold_in(stream_key, 1), (twos,), 0, 1 << 20) % (margin + 1)
    lengths = lengths.at[1:1 + 2 * twos:2].set(source_of - passed).at[2:2 + 2 * twos:2].set(sink + passed)
    return lengths[jax.random.permutation(jax.random.fold_in(stream_key, 2), number_of)]


def bell_draw(rng, extent, width, limit, shards=(), held_as=jnp.bfloat16):
    result = width * jax.random.normal(rng, extent, jnp.float32)
    if shards:
        result = result * block_scale(rng, extent, shards, -0.22, 0.18)
    return jnp.clip(result, -limit, limit).astype(held_as)


def gaussian_with(stream_key, extent, scale, bound, shards, heavy, kind=jnp.bfloat16):
    drawn = scale * jax.random.normal(stream_key, extent, jnp.float32)
    if shards:
        drawn = drawn * block_scale(stream_key, extent, shards, -0.22, 0.18)
    return jnp.clip(raised(drawn, jax.random.fold_in(stream_key, 3), *heavy), -bound, bound).astype(kind)


def setup_inputs(seed: int = 0) -> dict:
    key_list = jax.random.split(jax.random.key(seed), 8)
    return {
        "teacher_hidden": bell_draw(key_list[0], (TOKENS, DT), 1.0, 6.0, ((0, 4), (1, 4))),
        "teacher_gain": jnp.clip(1.0 + 0.15 * jax.random.normal(key_list[1], (DT,), jnp.float32), 0.25, 1.75).astype(jnp.bfloat16),
        "teacher_value": bell_draw(key_list[2], (DT, KV), DT ** -0.5, 0.0625, ((0, 4), (1, 2))),
        "student_hidden": gaussian_with(key_list[3], (TOKENS, DS), 1.0, 6.0, ((0, 16),), (0, 1, 16, 2.0)),
        "student_gain": jnp.clip(1.0 + 0.15 * jax.random.normal(key_list[4], (DS,), jnp.float32), 0.25, 1.75).astype(jnp.bfloat16),
        "student_value": bell_draw(key_list[5], (DS, KV), DS ** -0.5, 0.09375, ((0, 16), (1, 2))),
        "segment_ids": jax.vmap(lambda own: jnp.searchsorted(jnp.cumsum(ragged_sizes(own, NSEG, LEN, MOST, 2)), jnp.arange(LEN), side="right"))(jax.random.split(key_list[6], ROWS)).reshape((ROWS, LEN)).astype(jnp.int32),
    }


norm_eps = 1e-05
power_eps = 1e-06

def row_gradient(teacher_row, student_row, segment_row, teacher_gain, teacher_value, student_gain, student_value):
    teacher_wide = teacher_row.astype(jnp.float32)
    scaled = (teacher_wide * teacher_gain.astype(jnp.float32)).astype(jnp.bfloat16)
    teacher_scale = lax.rsqrt(lax.optimization_barrier(jnp.mean(teacher_wide * teacher_wide, axis=1, keepdims=True)) + norm_eps)
    target = jnp.dot(scaled, teacher_value, preferred_element_type=jnp.float32) * teacher_scale
    target_power = lax.optimization_barrier(jnp.mean(target * target, axis=1, keepdims=True)) + power_eps
    student_wide = student_row.astype(jnp.float32)
    student_scale = lax.rsqrt(lax.optimization_barrier(jnp.mean(student_wide * student_wide, axis=1, keepdims=True)) + norm_eps)
    normed = (student_wide * student_scale * student_gain.astype(jnp.float32)).astype(jnp.bfloat16)
    states = jnp.dot(normed, student_value, preferred_element_type=jnp.float32)
    matches = segment_row[:, None] == jnp.arange(NSEG, dtype=jnp.int32)[None, :]
    counts = lax.optimization_barrier(jnp.sum(matches.astype(jnp.int32), axis=0))
    doc_length = lax.optimization_barrier(jnp.sum(jnp.where(matches, counts[None, :], 0), axis=1)).astype(jnp.float32)
    weighted = ((states - target) / (doc_length[:, None] * target_power)).astype(jnp.bfloat16)
    return jnp.dot(normed.T, weighted, preferred_element_type=jnp.float32)

def reference(teacher_hidden, teacher_gain, teacher_value, student_hidden, student_gain, student_value, segment_ids):
    teacher_rows = teacher_hidden.reshape(ROWS, LEN, DT)
    student_rows = student_hidden.reshape(ROWS, LEN, DS)

    def advance(running, items):
        teacher_row, student_row, segment_row = items
        update = row_gradient(teacher_row, student_row, segment_row, teacher_gain, teacher_value, student_gain, student_value)
        return (running + update, None)
    running, unused = lax.scan(advance, jnp.zeros((DS, KV), jnp.float32), (teacher_rows, student_rows, segment_ids))
    return running
```

```python
import math

import jax
import jax.numpy as jnp
from jax import lax
from jax.sharding import PartitionSpec as P

NSEG = 8

norm_eps = 1e-05
power_eps = 1e-06

HIDDEN_MAX = 6.0
GAIN_MAX = 1.75
TEACHER_VALUE_MAX = 0.0625
STUDENT_VALUE_MAX = 0.09375
HALF_MAX = 60000.0


def half_scale(bound):
    return 2.0 ** math.floor(math.log2(HALF_MAX / bound))


def solution(mesh):
    sizes = dict(mesh.shape)
    grp, dp, mp = sizes["grp"], sizes["dp"], sizes["mp"]
    cores = 2 if dp % 2 == 0 else 1
    chips = dp // cores

    def swap(value, axis, step):
        return lax.ppermute(value, axis, [(i, i ^ step) for i in range(sizes[axis])])

    def per_device(
        teacher_hidden,
        teacher_gain,
        teacher_value,
        student_hidden,
        student_gain,
        student_value,
        segment_ids,
    ):
        f32, bf16, f16 = jnp.float32, jnp.bfloat16, jnp.float16
        tok, ds = student_hidden.shape
        kv_part = student_value.shape[1]
        rows = student_value.shape[0]
        dt_part = teacher_hidden.shape[1]
        dt, kv = dt_part * mp, kv_part * grp
        member = lax.axis_index("mp")
        place = lax.axis_index("dp")
        chip, core = place // cores, place % cores

        column = {0: student_value}
        step = mp // 2
        while step:
            offsets = sorted(column)
            sent = jnp.concatenate([column[o] for o in offsets], axis=0)
            got = swap(sent, "mp", step)
            for i, o in enumerate(offsets):
                column[o ^ step] = got[i * rows : (i + 1) * rows]
            step //= 2

        student_wide = student_hidden.astype(f32)
        student_scale = lax.rsqrt(
            jnp.mean(student_wide * student_wide, axis=1, keepdims=True) + norm_eps
        )
        normed = (student_wide * student_scale * student_gain.astype(f32)).astype(bf16)
        wide = ds // chips
        features = [
            lax.dynamic_slice_in_dim(normed, (chip ^ j) * wide, wide, 1) for j in range(chips)
        ]
        features = [features[0]] + [
            swap(features[j], "dp", cores * j) for j in range(1, chips)
        ]

        teacher_factor = half_scale(dt_part * HIDDEN_MAX * GAIN_MAX * TEACHER_VALUE_MAX)
        order = sorted(range(1, mp), key=lambda k: -k) + [0]
        if mp == 4:
            order = [2, 3, 1, 0]
        gain = teacher_gain.astype(f32)
        projected, squares = None, None
        for k in order:
            block = lax.dynamic_slice_in_dim(teacher_hidden, (member ^ k) * tok, tok, 0)
            wide_block = block.astype(f32)
            part = jnp.dot(
                (wide_block * gain).astype(bf16), teacher_value, preferred_element_type=f32
            )
            square = jnp.sum(wide_block * wide_block, axis=1)
            if k:
                part = swap((part * teacher_factor).astype(f16), "mp", k).astype(f32)
                part = part * (1.0 / teacher_factor)
                square = swap(square, "mp", k)
            projected = part if projected is None else projected + part
            squares = square if squares is None else squares + square
        teacher_scale = lax.rsqrt(squares / dt + norm_eps)
        target = projected * teacher_scale[:, None]
        power_half = jnp.sum(target * target, axis=1)
        power = power_half
        for k in range(1, grp):
            power = power + swap(power_half, "grp", k)
        target_power = power / kv + power_eps

        gathered = jnp.zeros((mp, rows, kv_part), bf16)
        for o, block in column.items():
            gathered = lax.dynamic_update_slice(gathered, block[None], (member ^ o, 0, 0))
        gathered = gathered.reshape(mp * rows, kv_part)
        if cores == 2:
            other = swap(gathered, "dp", 1)
            first = jnp.where(core == 0, gathered, other)
            second = jnp.where(core == 0, other, gathered)
            gathered = jnp.concatenate([first, second], axis=0)
        states_factor = half_scale(GAIN_MAX * ds * STUDENT_VALUE_MAX)
        states = jnp.dot(features[0], gathered, preferred_element_type=f32)
        for j in range(1, chips):
            part = jnp.dot(features[j], gathered, preferred_element_type=f32)
            part = swap((part * states_factor).astype(f16), "dp", cores * j).astype(f32)
            states = states + part * (1.0 / states_factor)

        matches = segment_ids[:, :, None] == jnp.arange(NSEG, dtype=jnp.int32)[None, None, :]
        counts = jnp.sum(matches.astype(jnp.int32), axis=1)
        lengths = jnp.sum(jnp.where(matches, counts[:, None, :], 0), axis=2).reshape(-1)
        doc_length = lax.dynamic_slice_in_dim(lengths, member * tok, tok, 0).astype(f32)
        weighted = ((states - target) / (doc_length * target_power)[:, None]).astype(bf16)

        seen = [weighted] + [swap(weighted, "dp", cores * j) for j in range(1, chips)]
        seen = jnp.concatenate(seen, axis=0)
        held = jnp.concatenate(features, axis=0)
        narrow = wide // cores
        mine = lax.dynamic_slice_in_dim(held, core * narrow, narrow, 1)
        if cores == 2:
            theirs = lax.dynamic_slice_in_dim(held, (1 - core) * narrow, narrow, 1)
            mine = jnp.concatenate([mine, swap(theirs, "dp", 1)], axis=0)
            seen = jnp.concatenate([seen, swap(seen, "dp", 1)], axis=0)
        total = None
        for k in order:
            block = lax.dynamic_slice_in_dim(mine, (member ^ k) * rows, rows, 1)
            part = lax.dot_general(
                block, seen, (((0,), (0,)), ((), ())), preferred_element_type=f32
            )
            if k:
                part = swap(part.astype(bf16), "mp", k).astype(f32)
            total = part if total is None else total + part
        return total

    return jax.shard_map(
        per_device,
        mesh=mesh,
        in_specs=(
            P("dp", "mp"),
            P("mp"),
            P("mp", "grp"),
            P(("dp", "mp"), None),
            P(),
            P(("dp", "mp"), "grp"),
            P("dp", None),
        ),
        out_specs=P(("dp", "mp"), "grp"),
        check_vma=False,
    )
```

```python
import math

import jax
import jax.numpy as jnp
from jax import lax
from jax.experimental import pallas as pl
from jax.experimental.pallas import tpu as pltpu
from jax.sharding import PartitionSpec as P

NSEG = 8

norm_eps = 1e-05
power_eps = 1e-06

HIDDEN_MAX = 6.0
GAIN_MAX = 1.75
TEACHER_VALUE_MAX = 0.0625
STUDENT_VALUE_MAX = 0.09375
HALF_MAX = 60000.0


def half_scale(bound):
    return 2.0 ** math.floor(math.log2(HALF_MAX / bound))


VMEM_BYTES = 24 * 2**20
SQUARE_FACTOR = 1024.0
EXTRA_ROWS = 16


def call(kernel, scalars, arrays, in_hbm, out, scratch, name):
    arrays = [pltpu.with_memory_space_constraint(a, pltpu.HBM) for a in arrays[:in_hbm]] + list(
        arrays[in_hbm:]
    )
    return pl.pallas_call(
        kernel,
        out_shape=[pltpu.VMEM(shape, dtype) for shape, dtype in out],
        grid_spec=pltpu.PrefetchScalarGridSpec(
            num_scalar_prefetch=1,
            grid=(),
            in_specs=[pl.BlockSpec(memory_space=pltpu.HBM)] * in_hbm
            + [pl.BlockSpec(memory_space=pltpu.VMEM)] * (len(arrays) - in_hbm),
            out_specs=[pl.BlockSpec(memory_space=pltpu.VMEM)] * len(out),
            scratch_shapes=scratch,
        ),
        compiler_params=pltpu.CompilerParams(vmem_limit_bytes=VMEM_BYTES),
        cost_estimate=pl.CostEstimate(flops=1, bytes_accessed=1, transcendentals=0),
        name=name,
    )(scalars.astype(jnp.int32), *arrays)


def lane_sum(wide, lanes):
    for c in range(0, wide.shape[1], 128):
        lanes = lanes + wide[:, c : c + 128]
    return lanes


def prepare(places, student, student_gain, hidden, gain, value, chips, cores, dt, factor):
    number = places.shape[0] - 2
    tok, ds = student.shape
    depth, kv = value.shape
    wide = ds // (chips * cores)
    chunk = math.gcd(512, wide)
    deep = math.gcd(512, depth)
    pieces = 4 if tok % 64 == 0 else 1
    rows = tok // pieces
    shared = cores + chips - 1

    def kernel(places_ref, student_ref, hidden_ref, value_ref, student_gain_ref, gain_ref, *refs):
        feature_refs, out_refs = refs[:shared], refs[shared : shared + number]
        student_held, held, value_held, scaled, square_ref, sems = refs[shared + number :]
        student_copies = []
        for p in range(pieces):
            at = pl.ds(p * rows, rows)
            student_copies.append(
                pltpu.make_async_copy(student_ref.at[at], student_held.at[at], sems.at[p])
            )
            student_copies[-1].start()
        copies = []
        for i in range(number):
            at = pl.ds(pl.multiple_of(places_ref[i] * tok, tok), tok)
            copies.append(
                pltpu.make_async_copy(hidden_ref.at[at], held.at[i], sems.at[pieces + i])
            )
            copies[-1].start()
        value_copy = pltpu.make_async_copy(value_ref, value_held, sems.at[pieces + number])
        value_copy.start()

        def normalise_rows(r, _):
            at = pl.ds(pl.multiple_of(r * 16, 16), 16)
            lanes = jnp.zeros((16, 128), jnp.float32)
            for c in range(0, ds, chunk):
                part = student_held[at, c : c + chunk].astype(jnp.float32)
                lanes = lane_sum(part * part, lanes)
            mean = jnp.sum(lanes, axis=1, keepdims=True) * (1.0 / ds)
            scale = lax.rsqrt(mean + norm_eps)
            for n in range(chips * cores):
                j, h = n // cores, n % cores
                chip = jnp.bitwise_xor(places_ref[number], j)
                core = jnp.bitwise_xor(places_ref[number + 1], h)
                base = (chip * cores + core) * wide
                feature_ref = feature_refs[cores - 1 + j if j else h]
                to = pl.ds(pl.multiple_of((h * tok if j else 0) + r * 16, 16), 16)
                for c in range(0, wide, chunk):
                    src = pl.ds(pl.multiple_of(base + c, chunk), chunk)
                    part = student_held[at, src].astype(jnp.float32) * scale
                    part = part * student_gain_ref[:, src].astype(jnp.float32)
                    feature_ref[to, c : c + chunk] = part.astype(jnp.bfloat16)
            return 0

        for p, copy in enumerate(student_copies):
            copy.wait()
            lax.fori_loop(p * rows // 16, (p + 1) * rows // 16, normalise_rows, 0, unroll=2)

        for i in range(number):
            copies[i].wait()

            def scale_rows(r, _, i=i):
                at = pl.ds(pl.multiple_of(r * 16, 16), 16)
                to = pl.ds(pl.multiple_of(i * tok + r * 16, 16), 16)
                lanes = jnp.zeros((16, 128), jnp.float32)
                for c in range(0, depth, deep):
                    part = held[i, at, c : c + deep].astype(jnp.float32)
                    lanes = lane_sum(part * part, lanes)
                    part = part * gain_ref[:, c : c + deep].astype(jnp.float32)
                    scaled[to, c : c + deep] = part.astype(jnp.bfloat16)
                square_ref[to, :] = lanes
                return 0

            lax.fori_loop(0, tok // 16, scale_rows, 0, unroll=4)
        value_copy.wait()
        product = jnp.dot(scaled[...], value_held[...], preferred_element_type=jnp.float32)
        ones = jnp.ones((8, 128), jnp.bfloat16)
        across = (((1,), (1,)), ((), ()))
        rest = square_ref[...]
        square = jnp.zeros((8, number * tok), jnp.float32)
        for _ in range(3):
            piece = rest.astype(jnp.bfloat16)
            rest = rest - piece.astype(jnp.float32)
            square += lax.dot_general(ones, piece, across, preferred_element_type=jnp.float32)
        square = square * (SQUARE_FACTOR / dt)
        first = square.astype(jnp.bfloat16).astype(jnp.float32)
        rest = (square - first) * 256.0
        second = rest.astype(jnp.bfloat16).astype(jnp.float32)
        third = (rest - second) * 256.0
        row = lax.broadcasted_iota(jnp.int32, (8, number * tok), 0)
        split = jnp.where(row == 0, first, jnp.where(row == 1, second, third))
        for i, out_ref in enumerate(out_refs):
            out_ref[:tok, :] = product[i * tok : (i + 1) * tok, :] * factor
            out_ref[tok:, :] = jnp.zeros((EXTRA_ROWS, kv), jnp.float32)
            out_ref[tok : tok + 8, :tok] = split[:, i * tok : (i + 1) * tok]

    results = call(
        kernel,
        places,
        [student, hidden, value, student_gain.reshape(1, ds), gain.reshape(1, depth)],
        3,
        [((tok, wide), jnp.bfloat16)] * cores
        + [((cores * tok, wide), jnp.bfloat16)] * (chips - 1)
        + [((tok + EXTRA_ROWS, kv), jnp.float32)] * number,
        [
            pltpu.VMEM((tok, ds), jnp.bfloat16),
            pltpu.VMEM((number, tok, depth), jnp.bfloat16),
            pltpu.VMEM((depth, kv), jnp.bfloat16),
            pltpu.VMEM((number * tok, depth), jnp.bfloat16),
            pltpu.VMEM((number * tok, 128), jnp.float32),
            pltpu.SemaphoreType.DMA((pieces + number + 1,)),
        ],
        "prepare",
    )
    return results[:cores], results[cores:shared], results[shared:]


def states_part(columns, features, values, rows, factor):
    cores = len(values)
    tok, wide = features[0].shape[0] * len(features) // cores, features[0].shape[1]
    kv = values[0][0].shape[1]
    flat = [v for of_core in values for v in of_core]
    spots = [
        (h, n, b)
        for h, of_core in enumerate(values)
        for n, v in enumerate(of_core)
        for b in range(v.shape[0] // rows)
    ]
    each = len(values[0])
    per_core = len(spots) // cores
    place = [(h, 0) if len(features) == cores else (0, h * tok) for h in range(cores)]
    alone = len(features) < cores
    if rows % 128:
        total = jnp.zeros((tok, kv), jnp.float32)
        for i, (h, n, b) in enumerate(spots):
            at = (place[h][1], columns[i % per_core] * rows)
            part = lax.dynamic_slice(features[place[h][0]], at, (tok, rows))
            block = lax.slice_in_dim(values[h][n], b * rows, (b + 1) * rows)
            total += jnp.dot(part, block, preferred_element_type=jnp.float32)
        return total * factor, features[-1][-tok:]

    def kernel(columns_ref, *refs):
        feature_refs, refs = refs[: len(features)], refs[len(features) :]
        value_refs, out_refs = refs[: len(flat)], refs[len(flat) :]
        total = jnp.zeros((tok, kv), jnp.float32)
        for i, (h, n, b) in enumerate(spots):
            start = pl.multiple_of(columns_ref[i % per_core] * rows, rows)
            array, above = place[h]
            total += jnp.dot(
                feature_refs[array][above : above + tok, pl.ds(start, rows)],
                value_refs[h * each + n][b * rows : (b + 1) * rows, :],
                preferred_element_type=jnp.float32,
            )
        out_refs[0][...] = total * factor
        if alone:
            out_refs[1][...] = feature_refs[-1][-tok:, :]

    out = [((tok, kv), jnp.float32)] + [((tok, wide), jnp.bfloat16)] * alone
    results = call(kernel, columns, [*features, *flat], 0, out, [], "states_part")
    return results[0], results[1] if alone else features[-1]


def turned(columns, blocks, rows):
    number = columns.shape[0]
    tok = blocks[0].shape[0]

    def kernel(columns_ref, *refs):
        block_refs, out_ref = refs[:-1], refs[-1]
        for i in range(number):
            src = pl.ds(pl.multiple_of(columns_ref[i] * rows, rows), rows)
            for b, block_ref in enumerate(block_refs):
                out_ref[i * rows : (i + 1) * rows, b * tok : (b + 1) * tok] = block_ref[:tok, src].T

    out = [((number * rows, len(blocks) * tok), jnp.bfloat16)]
    return call(kernel, columns, blocks, 0, out, [], "turned")[0]


def gradient_blocks(held, seen, number):
    rows, tok = held.shape[0] // number, seen[0].shape[0]
    kv = seen[0].shape[1]

    def kernel(_, held_ref, *refs):
        seen_refs, out_refs = refs[: len(seen)], refs[len(seen) :]
        for i, out_ref in enumerate(out_refs):
            total = jnp.zeros((rows, kv), jnp.float32)
            for b, seen_ref in enumerate(seen_refs):
                total += jnp.dot(
                    held_ref[i * rows : (i + 1) * rows, b * tok : (b + 1) * tok],
                    seen_ref[...],
                    preferred_element_type=jnp.float32,
                )
            out_ref[...] = total.astype(out_ref.dtype)

    out = [((rows, kv), jnp.bfloat16)] * (number - 1) + [((rows, kv), jnp.float32)]
    return call(kernel, jnp.zeros(1), [held, *seen], 0, out, [], "gradient_blocks")


def solution(mesh):
    sizes = dict(mesh.shape)
    grp, dp, mp = sizes["grp"], sizes["dp"], sizes["mp"]
    cores = 2 if dp % 2 == 0 else 1
    chips = dp // cores

    def swap(value, axis, step):
        return lax.ppermute(value, axis, [(i, i ^ step) for i in range(sizes[axis])])

    def per_device(
        teacher_hidden,
        teacher_gain,
        teacher_value,
        student_hidden,
        student_gain,
        student_value,
        segment_ids,
    ):
        f32, bf16, f16 = jnp.float32, jnp.bfloat16, jnp.float16
        tok, ds = student_hidden.shape
        kv_part = student_value.shape[1]
        rows = student_value.shape[0]
        dt_part = teacher_hidden.shape[1]
        dt, kv = dt_part * mp, kv_part * grp
        member = lax.axis_index("mp")
        place = lax.axis_index("dp")
        chip, core = place // cores, place % cores

        pieces = {0: student_value}
        step = mp // 2
        while step:
            pieces[step] = swap(student_value, "mp", step)
            step //= 2

        teacher_factor = half_scale(dt * HIDDEN_MAX * GAIN_MAX * TEACHER_VALUE_MAX)
        order = list(range(1, mp)) + [0]
        own, others, parts = prepare(
            jnp.stack([member ^ k for k in order] + [chip, core]),
            student_hidden,
            student_gain,
            teacher_hidden,
            teacher_gain,
            teacher_value,
            chips,
            cores,
            dt,
            teacher_factor,
        )
        others = [swap(part, "dp", cores * (j + 1)) for j, part in enumerate(others)]
        *parts, kept = parts
        parts = [part.astype(f16) for part in parts]
        parts, pieces = lax.optimization_barrier((parts, pieces))
        received = [swap(part, "mp", k) for k, part in zip(order, parts)]

        first = list(pieces)
        later = []
        step = mp // 4
        while step:
            for o in [o for o in pieces if o >= 2 * step and o % (2 * step) == 0]:
                if o ^ step not in pieces:
                    pieces[o ^ step] = swap(pieces[o], "mp", step)
                    later.append(o ^ step)
            step //= 2
        gathered = [jnp.concatenate([pieces[o] for o in first], axis=0)]
        gathered += [pieces[o] for o in later]
        gathered[-1], received[0] = lax.optimization_barrier((gathered[-1], received[0]))
        gathered = [gathered]
        if cores == 2:
            gathered.append([swap(v, "dp", 1) for v in gathered[0]])

        columns = jnp.stack([member ^ o for o in first + later])
        states_factor = half_scale(GAIN_MAX * ds * STUDENT_VALUE_MAX)
        returned = [
            states_part(columns, [part], gathered, rows, states_factor) for part in others
        ]
        second = [part[1] for part in returned]
        returned = [part[0].astype(f16) for part in returned]
        returned = [swap(part, "dp", cores * (j + 1)) for j, part in enumerate(returned)]
        states, _ = states_part(columns, own, gathered, rows, states_factor)

        held = [own[0], *others]
        if cores == 2:
            held += [swap(part, "dp", 1) for part in [own[1], *second]]
        turn_order = jnp.stack([member ^ k for k in order])
        if rows % 128 == 0:
            held = turned(turn_order, held, rows)

        summed = kept
        for part in received:
            summed = summed + part.astype(f32)
        pieces = summed[tok : tok + 3, :tok]
        squares = pieces[0] + (pieces[1] + pieces[2] * (1.0 / 256.0)) * (1.0 / 256.0)
        teacher_scale = lax.rsqrt(squares * (1.0 / SQUARE_FACTOR) + norm_eps)
        projected = summed[:tok] * (1.0 / teacher_factor)
        target = projected * teacher_scale[:, None]
        power_half = jnp.sum(target * target, axis=1)
        power = power_half
        for k in range(1, grp):
            power = power + swap(power_half, "grp", k)
        target_power = power / kv + power_eps

        for part in returned:
            states = states + part.astype(f32)
        states = states * (1.0 / states_factor)

        matches = segment_ids[:, :, None] == jnp.arange(NSEG, dtype=jnp.int32)[None, None, :]
        counts = jnp.sum(matches.astype(jnp.int32), axis=1)
        lengths = jnp.sum(jnp.where(matches, counts[:, None, :], 0), axis=2).reshape(-1)
        doc_length = lax.dynamic_slice_in_dim(lengths, member * tok, tok, 0).astype(f32)
        weighted = ((states - target) / (doc_length * target_power)[:, None]).astype(bf16)

        seen = [weighted] + [swap(weighted, "dp", cores * j) for j in range(1, chips)]
        if cores == 2:
            seen += [swap(part, "dp", 1) for part in seen]
        if rows % 128:
            held = jnp.concatenate([part[:tok] for part in held], axis=0)
            seen = jnp.concatenate(seen, axis=0)
            parts = [
                lax.dot_general(
                    lax.dynamic_slice_in_dim(held, turn_order[i] * rows, rows, 1),
                    seen,
                    (((0,), (0,)), ((), ())),
                    preferred_element_type=f32,
                ).astype(bf16 if order[i] else f32)
                for i in range(mp)
            ]
        else:
            parts = gradient_blocks(held, seen, mp)
        total = parts[-1]
        for i in range(mp - 1):
            total = total + swap(parts[i], "mp", order[i]).astype(f32)
        return total

    return jax.shard_map(
        per_device,
        mesh=mesh,
        in_specs=(
            P("dp", "mp"),
            P("mp"),
            P("mp", "grp"),
            P(("dp", "mp"), None),
            P(),
            P(("dp", "mp"), "grp"),
            P("dp", None),
        ),
        out_specs=P(("dp", "mp"), "grp"),
        check_vma=False,
    )
```

```python
import math

import jax
import jax.numpy as jnp
from jax import lax
from jax.experimental import pallas as pl
from jax.experimental.pallas import tpu as pltpu
from jax.sharding import PartitionSpec as P

NSEG = 8

norm_eps = 1e-05
power_eps = 1e-06

HIDDEN_MAX = 6.0
GAIN_MAX = 1.75
TEACHER_VALUE_MAX = 0.0625
STUDENT_VALUE_MAX = 0.09375
HALF_MAX = 60000.0


def half_scale(bound):
    return 2.0 ** math.floor(math.log2(HALF_MAX / bound))


VMEM_BYTES = 24 * 2**20
SQUARE_FACTOR = 1024.0
EXTRA_ROWS = 8


def call(kernel, scalars, arrays, in_hbm, out, scratch, name, out_hbm=()):
    arrays = [pltpu.with_memory_space_constraint(a, pltpu.HBM) for a in arrays[:in_hbm]] + list(
        arrays[in_hbm:]
    )
    return pl.pallas_call(
        kernel,
        out_shape=[
            (pltpu.HBM if n in out_hbm else pltpu.VMEM)(*leaf) for n, leaf in enumerate(out)
        ],
        grid_spec=pltpu.PrefetchScalarGridSpec(
            num_scalar_prefetch=1,
            grid=(),
            in_specs=[pl.BlockSpec(memory_space=pltpu.HBM)] * in_hbm
            + [pl.BlockSpec(memory_space=pltpu.VMEM)] * (len(arrays) - in_hbm),
            out_specs=[
                pl.BlockSpec(memory_space=pltpu.HBM if n in out_hbm else pltpu.VMEM)
                for n in range(len(out))
            ],
            scratch_shapes=scratch,
        ),
        compiler_params=pltpu.CompilerParams(vmem_limit_bytes=VMEM_BYTES),
        cost_estimate=pl.CostEstimate(flops=1, bytes_accessed=1, transcendentals=0),
        name=name,
    )(scalars.astype(jnp.int32), *arrays)


def lane_sum(wide, lanes):
    for c in range(0, wide.shape[1], 128):
        lanes = lanes + wide[:, c : c + 128]
    return lanes


def prepare(places, student, student_gain, hidden, gain, value, chips, cores, dt, factor):
    number = places.shape[0] - 2
    tok, ds = student.shape
    depth, kv = value.shape
    wide = ds // (chips * cores)
    chunk = math.gcd(512, wide)
    deep = math.gcd(512, depth)
    pieces = 4 if tok % 64 == 0 else 1
    rows = tok // pieces
    shared = cores + chips - 1

    def kernel(places_ref, student_ref, hidden_ref, value_ref, student_gain_ref, gain_ref, *refs):
        feature_refs, out_refs = refs[:shared], refs[shared : shared + number]
        student_held, held, value_held, scaled, square_ref, sems = refs[shared + number :]
        student_copies = []
        for p in range(pieces):
            at = pl.ds(p * rows, rows)
            student_copies.append(
                pltpu.make_async_copy(student_ref.at[at], student_held.at[at], sems.at[p])
            )
            student_copies[-1].start()
        copies = []
        for i in range(number):
            at = pl.ds(pl.multiple_of(places_ref[i] * tok, tok), tok)
            copies.append(
                pltpu.make_async_copy(hidden_ref.at[at], held.at[i], sems.at[pieces + i])
            )
            copies[-1].start()
        value_copy = pltpu.make_async_copy(value_ref, value_held, sems.at[pieces + number])
        value_copy.start()

        def normalise_rows(r, _):
            at = pl.ds(pl.multiple_of(r * 16, 16), 16)
            lanes = jnp.zeros((16, 128), jnp.float32)
            for c in range(0, ds, chunk):
                part = student_held[at, c : c + chunk].astype(jnp.float32)
                lanes = lane_sum(part * part, lanes)
            mean = jnp.sum(lanes, axis=1, keepdims=True) * (1.0 / ds)
            scale = lax.rsqrt(mean + norm_eps)
            for n in range(chips * cores):
                j, h = n // cores, n % cores
                chip = jnp.bitwise_xor(places_ref[number], j)
                core = jnp.bitwise_xor(places_ref[number + 1], h)
                base = (chip * cores + core) * wide
                feature_ref = feature_refs[cores - 1 + j if j else h]
                to = pl.ds(pl.multiple_of((h * tok if j else 0) + r * 16, 16), 16)
                for c in range(0, wide, chunk):
                    src = pl.ds(pl.multiple_of(base + c, chunk), chunk)
                    part = student_held[at, src].astype(jnp.float32) * scale
                    part = part * student_gain_ref[:, src].astype(jnp.float32)
                    feature_ref[to, c : c + chunk] = part.astype(jnp.bfloat16)
            return 0

        for p, copy in enumerate(student_copies):
            copy.wait()
            lax.fori_loop(p * rows // 16, (p + 1) * rows // 16, normalise_rows, 0, unroll=2)

        for i in range(number):
            copies[i].wait()

            def scale_rows(r, _, i=i):
                at = pl.ds(pl.multiple_of(r * 16, 16), 16)
                to = pl.ds(pl.multiple_of(i * tok + r * 16, 16), 16)
                lanes = jnp.zeros((16, 128), jnp.float32)
                for c in range(0, depth, deep):
                    part = held[i, at, c : c + deep].astype(jnp.float32)
                    lanes = lane_sum(part * part, lanes)
                    part = part * gain_ref[:, c : c + deep].astype(jnp.float32)
                    scaled[to, c : c + deep] = part.astype(jnp.bfloat16)
                square_ref[to, :] = lanes
                return 0

            lax.fori_loop(0, tok // 16, scale_rows, 0, unroll=4)
        value_copy.wait()
        product = jnp.dot(scaled[...], value_held[...], preferred_element_type=jnp.float32)
        ones = jnp.ones((8, 128), jnp.bfloat16)
        across = (((1,), (1,)), ((), ()))
        rest = square_ref[...]
        square = jnp.zeros((8, number * tok), jnp.float32)
        for _ in range(3):
            piece = rest.astype(jnp.bfloat16)
            rest = rest - piece.astype(jnp.float32)
            square += lax.dot_general(ones, piece, across, preferred_element_type=jnp.float32)
        square = square * (SQUARE_FACTOR / dt)
        first = square.astype(jnp.bfloat16).astype(jnp.float32)
        rest = (square - first) * 256.0
        second = rest.astype(jnp.bfloat16).astype(jnp.float32)
        third = (rest - second) * 256.0
        row = lax.broadcasted_iota(jnp.int32, (8, number * tok), 0)
        split = jnp.where(row == 0, first, jnp.where(row == 1, second, third))
        for i, out_ref in enumerate(out_refs):
            out_ref[:tok, :] = product[i * tok : (i + 1) * tok, :] * factor
            out_ref[tok:, :] = jnp.zeros((EXTRA_ROWS, kv), jnp.float32)
            out_ref[tok : tok + 8, :tok] = split[:, i * tok : (i + 1) * tok]

    results = call(
        kernel,
        places,
        [student, hidden, value, student_gain.reshape(1, ds), gain.reshape(1, depth)],
        3,
        [((tok, wide), jnp.bfloat16)] * cores
        + [((cores * tok, wide), jnp.bfloat16)] * (chips - 1)
        + [((tok + EXTRA_ROWS, kv), jnp.float32)] * number,
        [
            pltpu.VMEM((tok, ds), jnp.bfloat16),
            pltpu.VMEM((number, tok, depth), jnp.bfloat16),
            pltpu.VMEM((depth, kv), jnp.bfloat16),
            pltpu.VMEM((number * tok, depth), jnp.bfloat16),
            pltpu.VMEM((number * tok, 128), jnp.float32),
            pltpu.SemaphoreType.DMA((pieces + number + 1,)),
        ],
        "prepare",
    )
    return results[:cores], results[cores:shared], results[shared:]


def states_parts(columns, features, values, rows, factor):
    cores, chips = len(values), len(features)
    tok, wide = features[0][0].shape
    kv = values[0][0].shape[1]
    flat = [v for of_core in values for v in of_core]
    spots = [
        (h, n, b)
        for h, of_core in enumerate(values)
        for n, v in enumerate(of_core)
        for b in range(v.shape[0] // rows)
    ]
    each = len(values[0])
    per_core = len(spots) // cores
    arrays = [part for of_chip in features for part in of_chip]
    place, first = [], 0
    for of_chip in features:
        split = len(of_chip) == cores
        place.append([(first + h, 0) if split else (first, h * tok) for h in range(cores)])
        first += len(of_chip)
    alone = [first for first, of_chip in enumerate(features) if len(of_chip) < cores]
    if rows % 128:
        totals = []
        for j in range(chips):
            total = jnp.zeros((tok, kv), jnp.float32)
            for i, (h, n, b) in enumerate(spots):
                array, above = place[j][h]
                at = (above, columns[i % per_core] * rows)
                part = lax.dynamic_slice(arrays[array], at, (tok, rows))
                block = lax.slice_in_dim(values[h][n], b * rows, (b + 1) * rows)
                total += jnp.dot(part, block, preferred_element_type=jnp.float32)
            totals.append(total * factor)
        return totals, [features[j][-1][-tok:] for j in alone]

    def kernel(columns_ref, *refs):
        feature_refs, refs = refs[: len(arrays)], refs[len(arrays) :]
        value_refs, refs = refs[: len(flat)], refs[len(flat) :]
        out_refs, (own_ref, sems) = refs[:-2], refs[-2:]
        copies = []
        for n, j in enumerate(alone):
            src = feature_refs[place[j][0][0]].at[pl.ds((cores - 1) * tok, tok)]
            copies.append(pltpu.make_async_copy(src, out_refs[chips + n], sems.at[1 + n]))
            copies[-1].start()
        for j in range(chips):
            total = jnp.zeros((tok, kv), jnp.float32)
            for i, (h, n, b) in enumerate(spots):
                start = pl.multiple_of(columns_ref[i % per_core] * rows, rows)
                array, above = place[j][h]
                total += jnp.dot(
                    feature_refs[array][above : above + tok, pl.ds(start, rows)],
                    value_refs[h * each + n][b * rows : (b + 1) * rows, :],
                    preferred_element_type=jnp.float32,
                )
            if j:
                out_refs[j][...] = total * factor
            else:
                own_ref[...] = total * factor
                copies.append(pltpu.make_async_copy(own_ref, out_refs[0], sems.at[0]))
                copies[-1].start()
        for copy in copies:
            copy.wait()

    out = [((tok, kv), jnp.float32)] * chips + [((tok, wide), jnp.bfloat16)] * len(alone)
    scratch = [pltpu.VMEM((tok, kv), jnp.float32), pltpu.SemaphoreType.DMA((1 + len(alone),))]
    out_hbm = (0, *range(chips, len(out)))
    results = call(kernel, columns, [*arrays, *flat], 0, out, scratch, "states_parts", out_hbm)
    return results[:chips], results[chips:]


def turned(columns, blocks, rows):
    number = columns.shape[0]
    tok = blocks[0].shape[0]

    def kernel(columns_ref, *refs):
        block_refs, out_ref = refs[:-1], refs[-1]
        for i in range(number):
            src = pl.ds(pl.multiple_of(columns_ref[i] * rows, rows), rows)
            for b, block_ref in enumerate(block_refs):
                out_ref[i * rows : (i + 1) * rows, b * tok : (b + 1) * tok] = block_ref[:tok, src].T

    out = [((number * rows, len(blocks) * tok), jnp.bfloat16)]
    return call(kernel, columns, blocks, 0, out, [], "turned")[0]


def gradient_blocks(held, seen, number, rounded):
    rows, tok = held.shape[0] // number, seen[0].shape[0]
    kv = seen[0].shape[1]

    def kernel(_, held_ref, *refs):
        seen_refs, out_refs = refs[: len(seen)], refs[len(seen) :]
        for i, out_ref in enumerate(out_refs):
            total = jnp.zeros((rows, kv), jnp.float32)
            for b, seen_ref in enumerate(seen_refs):
                total += jnp.dot(
                    held_ref[i * rows : (i + 1) * rows, b * tok : (b + 1) * tok],
                    seen_ref[...],
                    preferred_element_type=jnp.float32,
                )
            out_ref[...] = total.astype(out_ref.dtype)

    out = [((rows, kv), jnp.bfloat16)] * rounded + [((rows, kv), jnp.float32)] * (number - rounded)
    return call(kernel, jnp.zeros(1), [held, *seen], 0, out, [], "gradient_blocks")


def solution(mesh):
    sizes = dict(mesh.shape)
    grp, dp, mp = sizes["grp"], sizes["dp"], sizes["mp"]
    cores = 2 if dp % 2 == 0 else 1
    chips = dp // cores

    def swap(value, axis, step):
        return lax.ppermute(value, axis, [(i, i ^ step) for i in range(sizes[axis])])

    def per_device(
        teacher_hidden,
        teacher_gain,
        teacher_value,
        student_hidden,
        student_gain,
        student_value,
        segment_ids,
    ):
        f32, bf16, f16 = jnp.float32, jnp.bfloat16, jnp.float16
        tok, ds = student_hidden.shape
        kv_part = student_value.shape[1]
        rows = student_value.shape[0]
        dt_part = teacher_hidden.shape[1]
        dt, kv = dt_part * mp, kv_part * grp
        member = lax.axis_index("mp")
        place = lax.axis_index("dp")
        chip, core = place // cores, place % cores

        pieces = {0: student_value}
        step = mp // 2
        while step:
            pieces[step] = swap(student_value, "mp", step)
            step //= 2

        teacher_factor = half_scale(dt * HIDDEN_MAX * GAIN_MAX * TEACHER_VALUE_MAX)
        order = list(range(1, mp)) + [0]
        own, others, parts = prepare(
            jnp.stack([member ^ k for k in order] + [chip, core]),
            student_hidden,
            student_gain,
            teacher_hidden,
            teacher_gain,
            teacher_value,
            chips,
            cores,
            dt,
            teacher_factor,
        )
        others = [swap(part, "dp", cores * (j + 1)) for j, part in enumerate(others)]
        *parts, kept = parts
        parts = [part.astype(f16) for part in parts]
        parts, pieces = lax.optimization_barrier((parts, pieces))
        received = [swap(part, "mp", k) for k, part in zip(order, parts)]

        first = list(pieces)
        later = []
        step = mp // 4
        while step:
            for o in [o for o in pieces if o >= 2 * step and o % (2 * step) == 0]:
                if o ^ step not in pieces:
                    pieces[o ^ step] = swap(pieces[o], "mp", step)
                    later.append(o ^ step)
            step //= 2
        gathered = [jnp.concatenate([pieces[o] for o in first], axis=0)]
        gathered += [pieces[o] for o in later]
        gathered[-1], received[0] = lax.optimization_barrier((gathered[-1], received[0]))
        gathered = [gathered]
        if cores == 2:
            gathered.append([swap(v, "dp", 1) for v in gathered[0]])

        columns = jnp.stack([member ^ o for o in first + later])
        states_factor = half_scale(GAIN_MAX * ds * STUDENT_VALUE_MAX)
        (states, *returned), second = states_parts(
            columns, [own] + [[part] for part in others], gathered, rows, states_factor
        )
        if cores == 1:
            second = others
        returned = payload = [part.astype(f16) for part in returned]
        returned = [swap(part, "dp", cores * (j + 1)) for j, part in enumerate(returned)]

        held = [own[0], *others]
        if cores == 2:
            held += [swap(part, "dp", 1) for part in [own[1], *second]]
        line = mp == 4
        if line:
            inner = (member == 1) | (member == 2)
            turn_order = [(1, 3), (3, 2), (2, 1), (0, 0)]
            turn_order = [member ^ jnp.where(inner, i, o) for i, o in turn_order]
        else:
            turn_order = [member ^ k for k in order]
        turn_order = jnp.stack(turn_order)
        if rows % 128 == 0:
            held = turned(turn_order, held, rows)

        summed = kept
        for part in received:
            summed = summed + part.astype(f32)
        pieces = summed[tok : tok + 3, :tok]
        squares = pieces[0] + (pieces[1] + pieces[2] * (1.0 / 256.0)) * (1.0 / 256.0)
        teacher_scale = lax.rsqrt(squares * (1.0 / SQUARE_FACTOR) + norm_eps)
        projected = summed[:tok] * (1.0 / teacher_factor)
        target = projected * teacher_scale[:, None]
        power_half = jnp.sum(target * target, axis=1)
        power_half, payload = lax.optimization_barrier((power_half, payload))
        power = power_half
        for k in range(1, grp):
            power = power + swap(power_half, "grp", k)
        target_power = power / kv + power_eps

        for part in returned:
            states = states + part.astype(f32)
        states = states * (1.0 / states_factor)

        matches = segment_ids[:, :, None] == jnp.arange(NSEG, dtype=jnp.int32)[None, None, :]
        counts = jnp.sum(matches.astype(jnp.int32), axis=1)
        lengths = jnp.sum(jnp.where(matches, counts[:, None, :], 0), axis=2).reshape(-1)
        doc_length = lax.dynamic_slice_in_dim(lengths, member * tok, tok, 0).astype(f32)
        weighted = ((states - target) / (doc_length * target_power)[:, None]).astype(bf16)

        seen = [swap(weighted, "dp", cores * j) for j in range(1, chips)]
        held, seen = lax.optimization_barrier((held, seen))
        seen = [weighted] + seen
        if cores == 2:
            seen += [swap(part, "dp", 1) for part in seen]
        rounded = 2 if line else mp - 1
        if rows % 128:
            held = jnp.concatenate([part[:tok] for part in held], axis=0)
            seen = jnp.concatenate(seen, axis=0)
            parts = [
                lax.dot_general(
                    lax.dynamic_slice_in_dim(held, turn_order[i] * rows, rows, 1),
                    seen,
                    (((0,), (0,)), ((), ())),
                    preferred_element_type=f32,
                )
                for i in range(mp)
            ]
            parts = [p.astype(bf16) for p in parts[:rounded]] + parts[rounded:]
        else:
            parts = gradient_blocks(held, seen, mp, rounded)
        if line:
            near = swap(parts[0], "mp", 1).astype(f32)
            across = lax.ppermute(parts[1], "mp", [(1, 2), (2, 1)])
            past = lax.ppermute(parts[1], "mp", [(0, 2), (3, 1)])
            last = (parts[2] + jnp.where(inner, near, 0.0)).astype(bf16)
            last = lax.ppermute(last, "mp", [(1, 3), (2, 0), (0, 1), (3, 2)])
            total = parts[3] + jnp.where(inner, 0.0, near)
            total = total + across.astype(f32) + past.astype(f32) + last.astype(f32)
        else:
            total = parts[-1]
            for i in range(mp - 1):
                total = total + swap(parts[i], "mp", order[i]).astype(f32)
        return total

    return jax.shard_map(
        per_device,
        mesh=mesh,
        in_specs=(
            P("dp", "mp"),
            P("mp"),
            P("mp", "grp"),
            P(("dp", "mp"), None),
            P(),
            P(("dp", "mp"), "grp"),
            P("dp", None),
        ),
        out_specs=P(("dp", "mp"), "grp"),
        check_vma=False,
    )
```

```python
import math

import jax
import jax.numpy as jnp
from jax import lax
from jax.experimental import pallas as pl
from jax.experimental.pallas import tpu as pltpu
from jax.sharding import PartitionSpec as P

NSEG = 8

norm_eps = 1e-05
power_eps = 1e-06

HIDDEN_MAX = 6.0
GAIN_MAX = 1.75
TEACHER_VALUE_MAX = 0.0625
STUDENT_VALUE_MAX = 0.09375
HALF_MAX = 60000.0


def half_scale(bound):
    return 2.0 ** math.floor(math.log2(HALF_MAX / bound))


VMEM_BYTES = 24 * 2**20
SQUARE_FACTOR = 1024.0
EXTRA_ROWS = 8


def call(kernel, scalars, arrays, in_hbm, out, scratch, name, out_hbm=()):
    arrays = [pltpu.with_memory_space_constraint(a, pltpu.HBM) for a in arrays[:in_hbm]] + list(
        arrays[in_hbm:]
    )
    return pl.pallas_call(
        kernel,
        out_shape=[
            (pltpu.HBM if n in out_hbm else pltpu.VMEM)(*leaf) for n, leaf in enumerate(out)
        ],
        grid_spec=pltpu.PrefetchScalarGridSpec(
            num_scalar_prefetch=1,
            grid=(),
            in_specs=[pl.BlockSpec(memory_space=pltpu.HBM)] * in_hbm
            + [pl.BlockSpec(memory_space=pltpu.VMEM)] * (len(arrays) - in_hbm),
            out_specs=[
                pl.BlockSpec(memory_space=pltpu.HBM if n in out_hbm else pltpu.VMEM)
                for n in range(len(out))
            ],
            scratch_shapes=scratch,
        ),
        compiler_params=pltpu.CompilerParams(vmem_limit_bytes=VMEM_BYTES),
        cost_estimate=pl.CostEstimate(flops=1, bytes_accessed=1, transcendentals=0),
        name=name,
    )(scalars.astype(jnp.int32), *arrays)


def lane_sum(wide, lanes):
    for c in range(0, wide.shape[1], 128):
        lanes = lanes + wide[:, c : c + 128]
    return lanes


def prepare(places, student, student_gain, hidden, gain, value, chips, cores, dt, factor):
    number = places.shape[0] - 2
    tok, ds = student.shape
    depth, kv = value.shape
    wide = ds // (chips * cores)
    chunk = math.gcd(512, wide)
    deep = math.gcd(512, depth)
    pieces = 4 if tok % 64 == 0 else 1
    rows = tok // pieces
    shared = cores + chips - 1

    def kernel(places_ref, student_ref, hidden_ref, value_ref, student_gain_ref, gain_ref, *refs):
        feature_outs, out_refs = refs[:shared], list(refs[shared : shared + number])
        student_held, held, value_held, scaled, square_ref, kept_ref, sems = refs[-7:]
        feature_refs = refs[shared + number : -7]
        kept_out, out_refs[-1] = out_refs[-1], kept_ref
        student_copies = []
        for p in range(pieces):
            at = pl.ds(p * rows, rows)
            student_copies.append(
                pltpu.make_async_copy(student_ref.at[at], student_held.at[at], sems.at[p])
            )
            student_copies[-1].start()
        copies = []
        for i in range(number):
            at = pl.ds(pl.multiple_of(places_ref[i] * tok, tok), tok)
            copies.append(
                pltpu.make_async_copy(hidden_ref.at[at], held.at[i], sems.at[pieces + i])
            )
            copies[-1].start()
        value_copy = pltpu.make_async_copy(value_ref, value_held, sems.at[pieces + number])
        value_copy.start()

        def normalise_rows(r, _):
            at = pl.ds(pl.multiple_of(r * 16, 16), 16)
            lanes = jnp.zeros((16, 128), jnp.float32)
            for c in range(0, ds, chunk):
                part = student_held[at, c : c + chunk].astype(jnp.float32)
                lanes = lane_sum(part * part, lanes)
            mean = jnp.sum(lanes, axis=1, keepdims=True) * (1.0 / ds)
            scale = lax.rsqrt(mean + norm_eps)
            for n in range(chips * cores):
                j, h = n // cores, n % cores
                chip = jnp.bitwise_xor(places_ref[number], j)
                core = jnp.bitwise_xor(places_ref[number + 1], h)
                base = (chip * cores + core) * wide
                feature_ref = feature_refs[cores - 1 + j if j else h]
                to = pl.ds(pl.multiple_of((h * tok if j else 0) + r * 16, 16), 16)
                for c in range(0, wide, chunk):
                    src = pl.ds(pl.multiple_of(base + c, chunk), chunk)
                    part = student_held[at, src].astype(jnp.float32) * scale
                    part = part * student_gain_ref[:, src].astype(jnp.float32)
                    feature_ref[to, c : c + chunk] = part.astype(jnp.bfloat16)
            return 0

        for p, copy in enumerate(student_copies):
            copy.wait()
            lax.fori_loop(p * rows // 16, (p + 1) * rows // 16, normalise_rows, 0, unroll=2)
        last = pieces + number + 1
        out_copies = []
        for n in range(shared):
            out_copies.append(
                pltpu.make_async_copy(feature_refs[n], feature_outs[n], sems.at[last + n])
            )
            out_copies[-1].start()

        for i in range(number):
            copies[i].wait()

            def scale_rows(r, _, i=i):
                at = pl.ds(pl.multiple_of(r * 16, 16), 16)
                to = pl.ds(pl.multiple_of(i * tok + r * 16, 16), 16)
                lanes = jnp.zeros((16, 128), jnp.float32)
                for c in range(0, depth, deep):
                    part = held[i, at, c : c + deep].astype(jnp.float32)
                    lanes = lane_sum(part * part, lanes)
                    part = part * gain_ref[:, c : c + deep].astype(jnp.float32)
                    scaled[to, c : c + deep] = part.astype(jnp.bfloat16)
                square_ref[to, :] = lanes
                return 0

            lax.fori_loop(0, tok // 16, scale_rows, 0, unroll=4)
        value_copy.wait()
        product = jnp.dot(scaled[...], value_held[...], preferred_element_type=jnp.float32)
        ones = jnp.ones((8, 128), jnp.bfloat16)
        across = (((1,), (1,)), ((), ()))
        rest = square_ref[...]
        square = jnp.zeros((8, number * tok), jnp.float32)
        for _ in range(3):
            piece = rest.astype(jnp.bfloat16)
            rest = rest - piece.astype(jnp.float32)
            square += lax.dot_general(ones, piece, across, preferred_element_type=jnp.float32)
        square = square * (SQUARE_FACTOR / dt)
        first = square.astype(jnp.bfloat16).astype(jnp.float32)
        rest = (square - first) * 256.0
        second = rest.astype(jnp.bfloat16).astype(jnp.float32)
        third = (rest - second) * 256.0
        row = lax.broadcasted_iota(jnp.int32, (8, number * tok), 0)
        split = jnp.where(row == 0, first, jnp.where(row == 1, second, third))
        for i, out_ref in enumerate(out_refs):
            out_ref[:tok, :] = product[i * tok : (i + 1) * tok, :] * factor
            out_ref[tok:, :] = jnp.zeros((EXTRA_ROWS, kv), jnp.float32)
            out_ref[tok : tok + 8, :tok] = split[:, i * tok : (i + 1) * tok]
        out_copies.append(pltpu.make_async_copy(kept_ref, kept_out, sems.at[last + shared]))
        out_copies[-1].start()
        for copy in out_copies:
            copy.wait()

    feature_shapes = [((tok, wide), jnp.bfloat16)] * cores
    feature_shapes += [((cores * tok, wide), jnp.bfloat16)] * (chips - 1)
    results = call(
        kernel,
        places,
        [student, hidden, value, student_gain.reshape(1, ds), gain.reshape(1, depth)],
        3,
        feature_shapes + [((tok + EXTRA_ROWS, kv), jnp.float32)] * number,
        [pltpu.VMEM(shape, dtype) for shape, dtype in feature_shapes]
        + [
            pltpu.VMEM((tok, ds), jnp.bfloat16),
            pltpu.VMEM((number, tok, depth), jnp.bfloat16),
            pltpu.VMEM((depth, kv), jnp.bfloat16),
            pltpu.VMEM((number * tok, depth), jnp.bfloat16),
            pltpu.VMEM((number * tok, 128), jnp.float32),
            pltpu.VMEM((tok + EXTRA_ROWS, kv), jnp.float32),
            pltpu.SemaphoreType.DMA((pieces + number + 2 + shared,)),
        ],
        "prepare",
        [*range(shared), shared + number - 1],
    )
    return results[:cores], results[cores:shared], results[shared:]


def states_parts(columns, features, values, rows, factor):
    cores, chips = len(values), len(features)
    tok, wide = features[0][0].shape
    kv = values[0][0].shape[1]
    flat = [v for of_core in values for v in of_core]
    spots = [
        (h, n, b)
        for h, of_core in enumerate(values)
        for n, v in enumerate(of_core)
        for b in range(v.shape[0] // rows)
    ]
    each = len(values[0])
    per_core = len(spots) // cores
    arrays = [part for of_chip in features for part in of_chip]
    place, first = [], 0
    for of_chip in features:
        split = len(of_chip) == cores
        place.append([(first + h, 0) if split else (first, h * tok) for h in range(cores)])
        first += len(of_chip)
    alone = [first for first, of_chip in enumerate(features) if len(of_chip) < cores]
    if rows % 128:
        totals = []
        for j in range(chips):
            total = jnp.zeros((tok, kv), jnp.float32)
            for i, (h, n, b) in enumerate(spots):
                array, above = place[j][h]
                at = (above, columns[i % per_core] * rows)
                part = lax.dynamic_slice(arrays[array], at, (tok, rows))
                block = lax.slice_in_dim(values[h][n], b * rows, (b + 1) * rows)
                total += jnp.dot(part, block, preferred_element_type=jnp.float32)
            totals.append(total * factor)
        return totals, [features[j][-1][-tok:] for j in alone]

    early = len(features[0])

    def kernel(columns_ref, *refs):
        own_refs, rest, refs = refs[:early], refs[early : len(arrays)], refs[len(arrays) :]
        value_refs, refs = refs[: len(flat)], refs[len(flat) :]
        out_refs, own_held, (own_ref, sems) = refs[: -2 - early], refs[-2 - early : -2], refs[-2:]
        own_copies = []
        for n in range(early):
            own_copies.append(pltpu.make_async_copy(own_refs[n], own_held[n], sems.at[n]))
            own_copies[-1].start()
        feature_refs = [*own_held, *rest]
        copies = []
        for n, j in enumerate(alone):
            src = feature_refs[place[j][0][0]].at[pl.ds((cores - 1) * tok, tok)]
            copies.append(pltpu.make_async_copy(src, out_refs[chips + n], sems.at[early + 1 + n]))
            copies[-1].start()
        for j in [*range(1, chips), 0]:
            if j == 0:
                for copy in own_copies:
                    copy.wait()
            total = jnp.zeros((tok, kv), jnp.float32)
            for i, (h, n, b) in enumerate(spots):
                start = pl.multiple_of(columns_ref[i % per_core] * rows, rows)
                array, above = place[j][h]
                total += jnp.dot(
                    feature_refs[array][above : above + tok, pl.ds(start, rows)],
                    value_refs[h * each + n][b * rows : (b + 1) * rows, :],
                    preferred_element_type=jnp.float32,
                )
            if j:
                out_refs[j][...] = total * factor
            else:
                out_refs[0][...] = total * factor
        for copy in copies:
            copy.wait()

    out = [((tok, kv), jnp.float32)] * chips + [((tok, wide), jnp.bfloat16)] * len(alone)
    scratch = [pltpu.VMEM(part.shape, part.dtype) for part in features[0]]
    scratch += [pltpu.VMEM((tok, kv), jnp.float32)]
    scratch += [pltpu.SemaphoreType.DMA((early + 1 + len(alone),))]
    out_hbm = range(chips, len(out))
    results = call(
        kernel, columns, [*arrays, *flat], early, out, scratch, "states_parts", out_hbm
    )
    return results[:chips], results[chips:]


def turned(columns, blocks, rows):
    number = columns.shape[0]
    tok = blocks[0].shape[0]

    def kernel(columns_ref, first_ref, *refs):
        block_refs, (out_ref, first_held, sem) = refs[:-3], refs[-3:]
        copy = pltpu.make_async_copy(first_ref, first_held, sem.at[0])
        copy.start()
        for b, block_ref in [*enumerate(block_refs, 1), (0, first_held)]:
            if b == 0:
                copy.wait()
            for i in range(number):
                src = pl.ds(pl.multiple_of(columns_ref[i] * rows, rows), rows)
                out_ref[i * rows : (i + 1) * rows, b * tok : (b + 1) * tok] = block_ref[:tok, src].T

    out = [((number * rows, len(blocks) * tok), jnp.bfloat16)]
    scratch = [pltpu.VMEM(blocks[0].shape, blocks[0].dtype), pltpu.SemaphoreType.DMA((1,))]
    return call(kernel, columns, blocks, 1, out, scratch, "turned")[0]


def gradient_blocks(held, seen, number, rounded):
    rows, tok = held.shape[0] // number, seen[0].shape[0]
    kv = seen[0].shape[1]

    def kernel(_, held_ref, *refs):
        seen_refs, out_refs = refs[: len(seen)], refs[len(seen) :]
        for i, out_ref in enumerate(out_refs):
            total = jnp.zeros((rows, kv), jnp.float32)
            for b, seen_ref in enumerate(seen_refs):
                total += jnp.dot(
                    held_ref[i * rows : (i + 1) * rows, b * tok : (b + 1) * tok],
                    seen_ref[...],
                    preferred_element_type=jnp.float32,
                )
            out_ref[...] = total.astype(out_ref.dtype)

    out = [((rows, kv), jnp.bfloat16)] * rounded + [((rows, kv), jnp.float32)] * (number - rounded)
    return call(kernel, jnp.zeros(1), [held, *seen], 0, out, [], "gradient_blocks")


def solution(mesh):
    sizes = dict(mesh.shape)
    grp, dp, mp = sizes["grp"], sizes["dp"], sizes["mp"]
    cores = 2 if dp % 2 == 0 else 1
    chips = dp // cores

    def swap(value, axis, step):
        return lax.ppermute(value, axis, [(i, i ^ step) for i in range(sizes[axis])])

    def per_device(
        teacher_hidden,
        teacher_gain,
        teacher_value,
        student_hidden,
        student_gain,
        student_value,
        segment_ids,
    ):
        f32, bf16, f16 = jnp.float32, jnp.bfloat16, jnp.float16
        tok, ds = student_hidden.shape
        kv_part = student_value.shape[1]
        rows = student_value.shape[0]
        dt_part = teacher_hidden.shape[1]
        dt, kv = dt_part * mp, kv_part * grp
        member = lax.axis_index("mp")
        place = lax.axis_index("dp")
        chip, core = place // cores, place % cores

        pieces = {0: student_value}
        step = mp // 2
        while step:
            pieces[step] = swap(student_value, "mp", step)
            step //= 2

        teacher_factor = half_scale(dt * HIDDEN_MAX * GAIN_MAX * TEACHER_VALUE_MAX)
        order = [2, 3, 1] + [0] if mp == 4 else list(range(1, mp)) + [0]
        own, others, parts = prepare(
            jnp.stack([member ^ k for k in order] + [chip, core]),
            student_hidden,
            student_gain,
            teacher_hidden,
            teacher_gain,
            teacher_value,
            chips,
            cores,
            dt,
            teacher_factor,
        )
        others = [swap(part, "dp", cores * (j + 1)) for j, part in enumerate(others)]
        *parts, kept = parts
        parts = [part.astype(f16) for part in parts]
        parts, pieces = lax.optimization_barrier((parts, pieces))
        received = [swap(part, "mp", k) for k, part in zip(order, parts)]

        first = list(pieces)
        later = []
        step = mp // 4
        while step:
            for o in [o for o in pieces if o >= 2 * step and o % (2 * step) == 0]:
                if o ^ step not in pieces:
                    pieces[o ^ step] = swap(pieces[o], "mp", step)
                    later.append(o ^ step)
            step //= 2
        gathered = [jnp.concatenate([pieces[o] for o in first], axis=0)]
        gathered += [pieces[o] for o in later]
        gathered[-1], received[2] = lax.optimization_barrier((gathered[-1], received[2]))
        gathered = [gathered]
        if cores == 2:
            gathered.append([swap(v, "dp", 1) for v in gathered[0]])

        columns = jnp.stack([member ^ o for o in first + later])
        states_factor = half_scale(GAIN_MAX * ds * STUDENT_VALUE_MAX)
        (states, *returned), second = states_parts(
            columns, [own] + [[part] for part in others], gathered, rows, states_factor
        )
        if cores == 1:
            second = others
        returned = payload = [part.astype(f16) for part in returned]
        returned = [swap(part, "dp", cores * (j + 1)) for j, part in enumerate(returned)]

        held = [own[0], *others]
        if cores == 2:
            held += [swap(part, "dp", 1) for part in [own[1], *second]]
        line = mp == 4
        if line:
            inner = (member == 1) | (member == 2)
            turn_order = [(1, 3), (3, 2), (2, 1), (0, 0)]
            turn_order = [member ^ jnp.where(inner, i, o) for i, o in turn_order]
        else:
            turn_order = [member ^ k for k in order]
        turn_order = jnp.stack(turn_order)
        if rows % 128 == 0:
            held = turned(turn_order, held, rows)

        summed = kept
        for part in received:
            summed = summed + part.astype(f32)
        pieces = summed[tok : tok + 3, :tok]
        squares = pieces[0] + (pieces[1] + pieces[2] * (1.0 / 256.0)) * (1.0 / 256.0)
        teacher_scale = lax.rsqrt(squares * (1.0 / SQUARE_FACTOR) + norm_eps)
        projected = summed[:tok] * (1.0 / teacher_factor)
        target = projected * teacher_scale[:, None]
        power_half = jnp.sum(target * target, axis=1)
        power_half, payload = lax.optimization_barrier((power_half, payload))
        power = power_half
        for k in range(1, grp):
            power = power + swap(power_half, "grp", k)
        target_power = power / kv + power_eps

        for part in returned:
            states = states + part.astype(f32)
        states = states * (1.0 / states_factor)

        matches = segment_ids[:, :, None] == jnp.arange(NSEG, dtype=jnp.int32)[None, None, :]
        counts = jnp.sum(matches.astype(jnp.int32), axis=1)
        lengths = jnp.sum(jnp.where(matches, counts[:, None, :], 0), axis=2).reshape(-1)
        doc_length = lax.dynamic_slice_in_dim(lengths, member * tok, tok, 0).astype(f32)
        weighted = ((states - target) / (doc_length * target_power)[:, None]).astype(bf16)

        seen = [swap(weighted, "dp", cores * j) for j in range(1, chips)]
        held, seen = lax.optimization_barrier((held, seen))
        seen = [weighted] + seen
        if cores == 2:
            seen += [swap(part, "dp", 1) for part in seen]
        rounded = 2 if line else mp - 1
        if rows % 128:
            held = jnp.concatenate([part[:tok] for part in held], axis=0)
            seen = jnp.concatenate(seen, axis=0)
            parts = [
                lax.dot_general(
                    lax.dynamic_slice_in_dim(held, turn_order[i] * rows, rows, 1),
                    seen,
                    (((0,), (0,)), ((), ())),
                    preferred_element_type=f32,
                )
                for i in range(mp)
            ]
            parts = [p.astype(bf16) for p in parts[:rounded]] + parts[rounded:]
        else:
            parts = gradient_blocks(held, seen, mp, rounded)
        if line:
            near = swap(parts[0], "mp", 1).astype(f32)
            past = lax.ppermute(parts[1], "mp", [(0, 2), (3, 1)])
            across = lax.ppermute(parts[1], "mp", [(1, 2), (2, 1)])
            last = (parts[2] + jnp.where(inner, near, 0.0)).astype(bf16)
            last = lax.ppermute(last, "mp", [(1, 3), (2, 0), (0, 1), (3, 2)])
            total = parts[3] + jnp.where(inner, 0.0, near)
            total = total + across.astype(f32) + past.astype(f32) + last.astype(f32)
        else:
            total = parts[-1]
            for i in range(mp - 1):
                total = total + swap(parts[i], "mp", order[i]).astype(f32)
        return total

    return jax.shard_map(
        per_device,
        mesh=mesh,
        in_specs=(
            P("dp", "mp"),
            P("mp"),
            P("mp", "grp"),
            P(("dp", "mp"), None),
            P(),
            P(("dp", "mp"), "grp"),
            P("dp", None),
        ),
        out_specs=P(("dp", "mp"), "grp"),
        check_vma=False,
    )
```

```python
import math

import jax
import jax.numpy as jnp
from jax import lax
from jax.experimental import pallas as pl
from jax.experimental.pallas import tpu as pltpu
from jax.sharding import PartitionSpec as P

NSEG = 8

norm_eps = 1e-05
power_eps = 1e-06

HIDDEN_MAX = 6.0
GAIN_MAX = 1.75
TEACHER_VALUE_MAX = 0.0625
STUDENT_VALUE_MAX = 0.09375
HALF_MAX = 60000.0


def half_scale(bound):
    return 2.0 ** math.floor(math.log2(HALF_MAX / bound))


VMEM_BYTES = 24 * 2**20
SQUARE_FACTOR = 1024.0
EXTRA_ROWS = 8


def call(kernel, scalars, arrays, in_hbm, out, scratch, name, out_hbm=()):
    arrays = [pltpu.with_memory_space_constraint(a, pltpu.HBM) for a in arrays[:in_hbm]] + list(
        arrays[in_hbm:]
    )
    return pl.pallas_call(
        kernel,
        out_shape=[
            (pltpu.HBM if n in out_hbm else pltpu.VMEM)(*leaf) for n, leaf in enumerate(out)
        ],
        grid_spec=pltpu.PrefetchScalarGridSpec(
            num_scalar_prefetch=1,
            grid=(),
            in_specs=[pl.BlockSpec(memory_space=pltpu.HBM)] * in_hbm
            + [pl.BlockSpec(memory_space=pltpu.VMEM)] * (len(arrays) - in_hbm),
            out_specs=[
                pl.BlockSpec(memory_space=pltpu.HBM if n in out_hbm else pltpu.VMEM)
                for n in range(len(out))
            ],
            scratch_shapes=scratch,
        ),
        compiler_params=pltpu.CompilerParams(vmem_limit_bytes=VMEM_BYTES),
        cost_estimate=pl.CostEstimate(flops=1, bytes_accessed=1, transcendentals=0),
        name=name,
    )(scalars.astype(jnp.int32), *arrays)


def lane_sum(wide, lanes):
    for c in range(0, wide.shape[1], 128):
        lanes = lanes + wide[:, c : c + 128]
    return lanes


def prepare(places, student, student_gain, hidden, gain, value, chips, cores, dt, factor):
    number = places.shape[0] - 2
    tok, ds = student.shape
    depth, kv = value.shape
    wide = ds // (chips * cores)
    chunk = math.gcd(512, wide)
    deep = math.gcd(512, depth)
    pieces = 4 if tok % 64 == 0 else 1
    rows = tok // pieces
    shared = cores + chips - 1

    def kernel(places_ref, student_ref, hidden_ref, value_ref, student_gain_ref, gain_ref, *refs):
        feature_outs, out_refs = refs[:shared], list(refs[shared : shared + number])
        student_held, held, value_held, scaled, square_ref, kept_ref, sems = refs[-7:]
        feature_refs = refs[shared + number : -7]
        kept_out, out_refs[-1] = out_refs[-1], kept_ref
        student_copies = []
        for p in range(pieces):
            at = pl.ds(p * rows, rows)
            student_copies.append(
                pltpu.make_async_copy(student_ref.at[at], student_held.at[at], sems.at[p])
            )
            student_copies[-1].start()
        copies = []
        for i in range(number):
            at = pl.ds(pl.multiple_of(places_ref[i] * tok, tok), tok)
            copies.append(
                pltpu.make_async_copy(hidden_ref.at[at], held.at[i], sems.at[pieces + i])
            )
            copies[-1].start()
        value_copy = pltpu.make_async_copy(value_ref, value_held, sems.at[pieces + number])
        value_copy.start()

        def normalise_rows(r, _):
            at = pl.ds(pl.multiple_of(r * 16, 16), 16)
            lanes = jnp.zeros((16, 128), jnp.float32)
            for c in range(0, ds, chunk):
                part = student_held[at, c : c + chunk].astype(jnp.float32)
                lanes = lane_sum(part * part, lanes)
            mean = jnp.sum(lanes, axis=1, keepdims=True) * (1.0 / ds)
            scale = lax.rsqrt(mean + norm_eps)
            for n in range(chips * cores):
                j, h = n // cores, n % cores
                chip = jnp.bitwise_xor(places_ref[number], j)
                core = jnp.bitwise_xor(places_ref[number + 1], h)
                base = (chip * cores + core) * wide
                feature_ref = feature_refs[cores - 1 + j if j else h]
                to = pl.ds(pl.multiple_of((h * tok if j else 0) + r * 16, 16), 16)
                for c in range(0, wide, chunk):
                    src = pl.ds(pl.multiple_of(base + c, chunk), chunk)
                    part = student_held[at, src].astype(jnp.float32) * scale
                    part = part * student_gain_ref[:, src].astype(jnp.float32)
                    feature_ref[to, c : c + chunk] = part.astype(jnp.bfloat16)
            return 0

        for p, copy in enumerate(student_copies):
            copy.wait()
            lax.fori_loop(p * rows // 16, (p + 1) * rows // 16, normalise_rows, 0, unroll=2)
        last = pieces + number + 1
        out_copies = []
        for n in range(shared):
            out_copies.append(
                pltpu.make_async_copy(feature_refs[n], feature_outs[n], sems.at[last + n])
            )
            out_copies[-1].start()

        for i in range(number):
            copies[i].wait()

            def scale_rows(r, _, i=i):
                at = pl.ds(pl.multiple_of(r * 16, 16), 16)
                to = pl.ds(pl.multiple_of(i * tok + r * 16, 16), 16)
                lanes = jnp.zeros((16, 128), jnp.float32)
                for c in range(0, depth, deep):
                    part = held[i, at, c : c + deep].astype(jnp.float32)
                    lanes = lane_sum(part * part, lanes)
                    part = part * gain_ref[:, c : c + deep].astype(jnp.float32)
                    scaled[to, c : c + deep] = part.astype(jnp.bfloat16)
                square_ref[to, :] = lanes
                return 0

            lax.fori_loop(0, tok // 16, scale_rows, 0, unroll=4)
        value_copy.wait()
        product = jnp.dot(scaled[...], value_held[...], preferred_element_type=jnp.float32)
        ones = jnp.ones((8, 128), jnp.bfloat16)
        across = (((1,), (1,)), ((), ()))
        rest = square_ref[...]
        square = jnp.zeros((8, number * tok), jnp.float32)
        for _ in range(3):
            piece = rest.astype(jnp.bfloat16)
            rest = rest - piece.astype(jnp.float32)
            square += lax.dot_general(ones, piece, across, preferred_element_type=jnp.float32)
        square = square * (SQUARE_FACTOR / dt)
        first = square.astype(jnp.bfloat16).astype(jnp.float32)
        rest = (square - first) * 256.0
        second = rest.astype(jnp.bfloat16).astype(jnp.float32)
        third = (rest - second) * 256.0
        row = lax.broadcasted_iota(jnp.int32, (8, number * tok), 0)
        split = jnp.where(row == 0, first, jnp.where(row == 1, second, third))
        for i, out_ref in enumerate(out_refs):
            out_ref[:tok, :] = product[i * tok : (i + 1) * tok, :] * factor
            out_ref[tok:, :] = jnp.zeros((EXTRA_ROWS, kv), jnp.float32)
            out_ref[tok : tok + 8, :tok] = split[:, i * tok : (i + 1) * tok]
        out_copies.append(pltpu.make_async_copy(kept_ref, kept_out, sems.at[last + shared]))
        out_copies[-1].start()
        for copy in out_copies:
            copy.wait()

    feature_shapes = [((tok, wide), jnp.bfloat16)] * cores
    feature_shapes += [((cores * tok, wide), jnp.bfloat16)] * (chips - 1)
    results = call(
        kernel,
        places,
        [student, hidden, value, student_gain.reshape(1, ds), gain.reshape(1, depth)],
        3,
        feature_shapes + [((tok + EXTRA_ROWS, kv), jnp.float32)] * number,
        [pltpu.VMEM(shape, dtype) for shape, dtype in feature_shapes]
        + [
            pltpu.VMEM((tok, ds), jnp.bfloat16),
            pltpu.VMEM((number, tok, depth), jnp.bfloat16),
            pltpu.VMEM((depth, kv), jnp.bfloat16),
            pltpu.VMEM((number * tok, depth), jnp.bfloat16),
            pltpu.VMEM((number * tok, 128), jnp.float32),
            pltpu.VMEM((tok + EXTRA_ROWS, kv), jnp.float32),
            pltpu.SemaphoreType.DMA((pieces + number + 2 + shared,)),
        ],
        "prepare",
        [*range(shared), shared + number - 1],
    )
    return results[:cores], results[cores:shared], results[shared:]


def states_parts(columns, features, values, rows, factor, early):
    cores, chips = len(values), len(features)
    tok, wide = features[0][0].shape
    tok = tok * len(features[0]) // cores
    kv = values[0][0].shape[1]
    flat = [v for of_core in values for v in of_core]
    spots = [
        (h, n, b)
        for h, of_core in enumerate(values)
        for n, v in enumerate(of_core)
        for b in range(v.shape[0] // rows)
    ]
    each = len(values[0])
    per_core = len(spots) // cores
    arrays = [part for of_chip in features for part in of_chip]
    place, first = [], 0
    for of_chip in features:
        split = len(of_chip) == cores
        place.append([(first + h, 0) if split else (first, h * tok) for h in range(cores)])
        first += len(of_chip)
    alone = [first for first, of_chip in enumerate(features) if len(of_chip) < cores]
    if rows % 128:
        totals = []
        for j in range(chips):
            total = jnp.zeros((tok, kv), jnp.float32)
            for i, (h, n, b) in enumerate(spots):
                array, above = place[j][h]
                at = (above, columns[i % per_core] * rows)
                part = lax.dynamic_slice(arrays[array], at, (tok, rows))
                block = lax.slice_in_dim(values[h][n], b * rows, (b + 1) * rows)
                total += jnp.dot(part, block, preferred_element_type=jnp.float32)
            totals.append(total * factor)
        return totals, [features[j][-1][-tok:] for j in alone]


    def kernel(columns_ref, *refs):
        own_refs, rest, refs = refs[:early], refs[early : len(arrays)], refs[len(arrays) :]
        value_refs, refs = refs[: len(flat)], refs[len(flat) :]
        out_refs, own_held, (own_ref, sems) = refs[: -2 - early], refs[-2 - early : -2], refs[-2:]
        own_copies = []
        for n in range(early):
            own_copies.append(pltpu.make_async_copy(own_refs[n], own_held[n], sems.at[n]))
            own_copies[-1].start()
        feature_refs = [*own_held, *rest]
        copies = []
        for n, j in enumerate(alone):
            src = feature_refs[place[j][0][0]].at[pl.ds((cores - 1) * tok, tok)]
            copies.append(pltpu.make_async_copy(src, out_refs[chips + n], sems.at[early + 1 + n]))
            copies[-1].start()
        for j in range(chips):
            if j == 0:
                for copy in own_copies:
                    copy.wait()
            total = jnp.zeros((tok, kv), jnp.float32)
            for i, (h, n, b) in enumerate(spots):
                start = pl.multiple_of(columns_ref[i % per_core] * rows, rows)
                array, above = place[j][h]
                total += jnp.dot(
                    feature_refs[array][above : above + tok, pl.ds(start, rows)],
                    value_refs[h * each + n][b * rows : (b + 1) * rows, :],
                    preferred_element_type=jnp.float32,
                )
            out_refs[j][...] = total * factor
        for copy in copies:
            copy.wait()

    out = [((tok, kv), jnp.float32)] * chips + [((tok, wide), jnp.bfloat16)] * len(alone)
    scratch = [pltpu.VMEM(part.shape, part.dtype) for part in arrays[:early]]
    scratch += [pltpu.VMEM((tok, kv), jnp.float32)]
    scratch += [pltpu.SemaphoreType.DMA((early + 1 + len(alone),))]
    out_hbm = range(chips, len(out))
    results = call(
        kernel, columns, [*arrays, *flat], early, out, scratch, "states_parts", out_hbm
    )
    return results[:chips], results[chips:]


def turned(columns, blocks, rows):
    number = columns.shape[0]
    tok = blocks[0].shape[0]

    def kernel(columns_ref, first_ref, *refs):
        block_refs, (out_ref, first_held, sem) = refs[:-3], refs[-3:]
        copy = pltpu.make_async_copy(first_ref, first_held, sem.at[0])
        copy.start()
        for b, block_ref in [*enumerate(block_refs, 1), (0, first_held)]:
            if b == 0:
                copy.wait()
            for i in range(number):
                src = pl.ds(pl.multiple_of(columns_ref[i] * rows, rows), rows)
                out_ref[i * rows : (i + 1) * rows, b * tok : (b + 1) * tok] = block_ref[:tok, src].T

    out = [((number * rows, len(blocks) * tok), jnp.bfloat16)]
    scratch = [pltpu.VMEM(blocks[0].shape, blocks[0].dtype), pltpu.SemaphoreType.DMA((1,))]
    return call(kernel, columns, blocks, 1, out, scratch, "turned")[0]


def gradient_blocks(held, seen, number, blocks, dtype):
    rows, tok = held.shape[0] // number, seen[0].shape[0]
    kv = seen[0].shape[1]

    def kernel(_, held_ref, *refs):
        seen_refs, out_refs = refs[: len(seen)], refs[len(seen) :]
        for i, out_ref in zip(blocks, out_refs):
            total = jnp.zeros((rows, kv), jnp.float32)
            for b, seen_ref in enumerate(seen_refs):
                total += jnp.dot(
                    held_ref[i * rows : (i + 1) * rows, b * tok : (b + 1) * tok],
                    seen_ref[...],
                    preferred_element_type=jnp.float32,
                )
            out_ref[...] = total.astype(out_ref.dtype)

    out = [((rows, kv), dtype)] * len(blocks)
    return call(kernel, jnp.zeros(1), [held, *seen], 0, out, [], "gradient_blocks")


def solution(mesh):
    sizes = dict(mesh.shape)
    grp, dp, mp = sizes["grp"], sizes["dp"], sizes["mp"]
    cores = 2 if dp % 2 == 0 else 1
    chips = dp // cores

    def swap(value, axis, step):
        return lax.ppermute(value, axis, [(i, i ^ step) for i in range(sizes[axis])])

    def per_device(
        teacher_hidden,
        teacher_gain,
        teacher_value,
        student_hidden,
        student_gain,
        student_value,
        segment_ids,
    ):
        f32, bf16, f16 = jnp.float32, jnp.bfloat16, jnp.float16
        tok, ds = student_hidden.shape
        kv_part = student_value.shape[1]
        rows = student_value.shape[0]
        dt_part = teacher_hidden.shape[1]
        dt, kv = dt_part * mp, kv_part * grp
        member = lax.axis_index("mp")
        place = lax.axis_index("dp")
        chip, core = place // cores, place % cores

        pieces = {0: student_value}
        step = mp // 2
        while step:
            pieces[step] = swap(student_value, "mp", step)
            step //= 2

        teacher_factor = half_scale(dt * HIDDEN_MAX * GAIN_MAX * TEACHER_VALUE_MAX)
        order = [2, 3, 1] + [0] if mp == 4 else list(range(1, mp)) + [0]
        own, others, parts = prepare(
            jnp.stack([member ^ k for k in order] + [chip, core]),
            student_hidden,
            student_gain,
            teacher_hidden,
            teacher_gain,
            teacher_value,
            chips,
            cores,
            dt,
            teacher_factor,
        )
        others = [swap(part, "dp", cores * (j + 1)) for j, part in enumerate(others)]
        *parts, kept = parts
        parts = [part.astype(f16) for part in parts]
        parts, pieces = lax.optimization_barrier((parts, pieces))
        received = [swap(part, "mp", k) for k, part in zip(order, parts)]

        first = list(pieces)
        later = []
        step = mp // 4
        while step:
            for o in [o for o in pieces if o >= 2 * step and o % (2 * step) == 0]:
                if o ^ step not in pieces:
                    pieces[o ^ step] = swap(pieces[o], "mp", step)
                    later.append(o ^ step)
            step //= 2
        gathered = [jnp.concatenate([pieces[o] for o in first], axis=0)]
        gathered += [pieces[o] for o in later]
        gathered[-1], received[2] = lax.optimization_barrier((gathered[-1], received[2]))
        gathered = [gathered]
        if cores == 2:
            gathered.append([swap(v, "dp", 1) for v in gathered[0]])

        columns = jnp.stack([member ^ o for o in first + later])
        states_factor = half_scale(GAIN_MAX * ds * STUDENT_VALUE_MAX)
        returned, second = states_parts(
            columns, [[part] for part in others], gathered, rows, states_factor, 0
        )
        (states,), _ = states_parts(columns, [own], gathered, rows, states_factor, len(own))
        if cores == 1:
            second = others
        returned = payload = [part.astype(f16) for part in returned]
        returned = [swap(part, "dp", cores * (j + 1)) for j, part in enumerate(returned)]

        held = [own[0], *others]
        if cores == 2:
            held += [swap(part, "dp", 1) for part in [own[1], *second]]
        line = mp == 4
        if line:
            inner = (member == 1) | (member == 2)
            turn_order = [(1, 3), (3, 2), (2, 1), (0, 0)]
            turn_order = [member ^ jnp.where(inner, i, o) for i, o in turn_order]
        else:
            turn_order = [member ^ k for k in order]
        turn_order = jnp.stack(turn_order)
        if rows % 128 == 0:
            held = turned(turn_order, held, rows)

        summed = kept
        for part in received:
            summed = summed + part.astype(f32)
        pieces = summed[tok : tok + 3, :tok]
        squares = pieces[0] + (pieces[1] + pieces[2] * (1.0 / 256.0)) * (1.0 / 256.0)
        teacher_scale = lax.rsqrt(squares * (1.0 / SQUARE_FACTOR) + norm_eps)
        projected = summed[:tok] * (1.0 / teacher_factor)
        target = projected * teacher_scale[:, None]
        power_half = jnp.sum(target * target, axis=1)
        power_half, payload = lax.optimization_barrier((power_half, payload))
        power = power_half
        for k in range(1, grp):
            power = power + swap(power_half, "grp", k)
        target_power = power / kv + power_eps

        for part in returned:
            states = states + part.astype(f32)
        states = states * (1.0 / states_factor)

        matches = segment_ids[:, :, None] == jnp.arange(NSEG, dtype=jnp.int32)[None, None, :]
        counts = jnp.sum(matches.astype(jnp.int32), axis=1)
        lengths = jnp.sum(jnp.where(matches, counts[:, None, :], 0), axis=2).reshape(-1)
        doc_length = lax.dynamic_slice_in_dim(lengths, member * tok, tok, 0).astype(f32)
        weighted = ((states - target) / (doc_length * target_power)[:, None]).astype(bf16)

        seen = [swap(weighted, "dp", cores * j) for j in range(1, chips)]
        held, seen = lax.optimization_barrier((held, seen))
        seen = [weighted] + seen
        if cores == 2:
            seen += [swap(part, "dp", 1) for part in seen]
        rounded = 2 if line else mp - 1
        if rows % 128:
            held = jnp.concatenate([part[:tok] for part in held], axis=0)
            seen = jnp.concatenate(seen, axis=0)
            parts = [
                lax.dot_general(
                    lax.dynamic_slice_in_dim(held, turn_order[i] * rows, rows, 1),
                    seen,
                    (((0,), (0,)), ((), ())),
                    preferred_element_type=f32,
                )
                for i in range(mp)
            ]
            parts = [p.astype(bf16) for p in parts[:rounded]] + parts[rounded:]
        else:
            parts = [
                *gradient_blocks(held, seen, mp, range(rounded), bf16),
                *gradient_blocks(held, seen, mp, range(rounded, mp), f32),
            ]
        if line:
            near = swap(parts[0], "mp", 1).astype(f32)
            past = lax.ppermute(parts[1], "mp", [(0, 2), (3, 1)])
            across = lax.ppermute(parts[1], "mp", [(1, 2), (2, 1)])
            last = (parts[2] + jnp.where(inner, near, 0.0)).astype(bf16)
            last = lax.ppermute(last, "mp", [(1, 3), (2, 0), (0, 1), (3, 2)])
            total = parts[3] + jnp.where(inner, 0.0, near)
            total = total + across.astype(f32) + past.astype(f32) + last.astype(f32)
        else:
            total = parts[-1]
            for i in range(mp - 1):
                total = total + swap(parts[i], "mp", order[i]).astype(f32)
        return total

    return jax.shard_map(
        per_device,
        mesh=mesh,
        in_specs=(
            P("dp", "mp"),
            P("mp"),
            P("mp", "grp"),
            P(("dp", "mp"), None),
            P(),
            P(("dp", "mp"), "grp"),
            P("dp", None),
        ),
        out_specs=P(("dp", "mp"), "grp"),
        check_vma=False,
    )
```

```python
import math

import jax
import jax.numpy as jnp
from jax import lax
from jax.experimental import pallas as pl
from jax.experimental.pallas import tpu as pltpu
from jax.sharding import PartitionSpec as P

NSEG = 8

norm_eps = 1e-05
power_eps = 1e-06

HIDDEN_MAX = 6.0
GAIN_MAX = 1.75
TEACHER_VALUE_MAX = 0.0625
STUDENT_VALUE_MAX = 0.09375
HALF_MAX = 60000.0


def half_scale(bound):
    return 2.0 ** math.floor(math.log2(HALF_MAX / bound))


VMEM_BYTES = 24 * 2**20
SQUARE_FACTOR = 1024.0
EXTRA_ROWS = 8


def call(kernel, scalars, arrays, in_hbm, out, scratch, name, out_hbm=()):
    arrays = [pltpu.with_memory_space_constraint(a, pltpu.HBM) for a in arrays[:in_hbm]] + list(
        arrays[in_hbm:]
    )
    return pl.pallas_call(
        kernel,
        out_shape=[
            (pltpu.HBM if n in out_hbm else pltpu.VMEM)(*leaf) for n, leaf in enumerate(out)
        ],
        grid_spec=pltpu.PrefetchScalarGridSpec(
            num_scalar_prefetch=1,
            grid=(),
            in_specs=[pl.BlockSpec(memory_space=pltpu.HBM)] * in_hbm
            + [pl.BlockSpec(memory_space=pltpu.VMEM)] * (len(arrays) - in_hbm),
            out_specs=[
                pl.BlockSpec(memory_space=pltpu.HBM if n in out_hbm else pltpu.VMEM)
                for n in range(len(out))
            ],
            scratch_shapes=scratch,
        ),
        compiler_params=pltpu.CompilerParams(vmem_limit_bytes=VMEM_BYTES),
        cost_estimate=pl.CostEstimate(flops=1, bytes_accessed=1, transcendentals=0),
        name=name,
    )(scalars.astype(jnp.int32), *arrays)


def lane_sum(wide, lanes):
    for c in range(0, wide.shape[1], 128):
        lanes = lanes + wide[:, c : c + 128]
    return lanes


def prepare(places, student, student_gain, hidden, gain, value, chips, cores, dt, factor):
    number = places.shape[0] - 2
    tok, ds = student.shape
    depth, kv = value.shape
    wide = ds // (chips * cores)
    chunk = math.gcd(512, wide)
    deep = math.gcd(512, depth)
    pieces = 4 if tok % 64 == 0 else 1
    rows = tok // pieces
    shared = cores + chips - 1

    def kernel(places_ref, student_ref, hidden_ref, value_ref, gains_ref, *refs):
        feature_outs, out_refs = refs[:shared], list(refs[shared : shared + number])
        student_held, held, value_held, scaled, square_ref, kept_ref, sems = refs[-7:]
        feature_refs = refs[shared + number : -7]
        kept_out, out_refs[-1] = out_refs[-1], kept_ref
        student_copies = []
        for p in range(pieces):
            at = pl.ds(p * rows, rows)
            student_copies.append(
                pltpu.make_async_copy(student_ref.at[at], student_held.at[at], sems.at[p])
            )
            student_copies[-1].start()
        copies = []
        for i in range(number):
            at = pl.ds(pl.multiple_of(places_ref[i] * tok, tok), tok)
            copies.append(
                pltpu.make_async_copy(hidden_ref.at[at], held.at[i], sems.at[pieces + i])
            )
            copies[-1].start()
        value_copy = pltpu.make_async_copy(value_ref, value_held, sems.at[pieces + number])
        value_copy.start()

        def normalise_rows(r, _):
            at = pl.ds(pl.multiple_of(r * 16, 16), 16)
            lanes = jnp.zeros((16, 128), jnp.float32)
            for c in range(0, ds, chunk):
                part = student_held[at, c : c + chunk].astype(jnp.float32)
                lanes = lane_sum(part * part, lanes)
            mean = jnp.sum(lanes, axis=1, keepdims=True) * (1.0 / ds)
            scale = lax.rsqrt(mean + norm_eps)
            for n in range(chips * cores):
                j, h = n // cores, n % cores
                chip = jnp.bitwise_xor(places_ref[number], j)
                core = jnp.bitwise_xor(places_ref[number + 1], h)
                base = (chip * cores + core) * wide
                feature_ref = feature_refs[cores - 1 + j if j else h]
                to = pl.ds(pl.multiple_of((h * tok if j else 0) + r * 16, 16), 16)
                for c in range(0, wide, chunk):
                    src = pl.ds(pl.multiple_of(base + c, chunk), chunk)
                    part = student_held[at, src].astype(jnp.float32) * scale
                    part = part * gains_ref[:, src].astype(jnp.float32)
                    feature_ref[to, c : c + chunk] = part.astype(jnp.bfloat16)
            return 0

        for p, copy in enumerate(student_copies):
            copy.wait()
            lax.fori_loop(p * rows // 16, (p + 1) * rows // 16, normalise_rows, 0, unroll=2)
        last = pieces + number + 1
        out_copies = []
        for n in range(shared):
            out_copies.append(
                pltpu.make_async_copy(feature_refs[n], feature_outs[n], sems.at[last + n])
            )
            out_copies[-1].start()

        for i in range(number):
            copies[i].wait()

            def scale_rows(r, _, i=i):
                at = pl.ds(pl.multiple_of(r * 16, 16), 16)
                to = pl.ds(pl.multiple_of(i * tok + r * 16, 16), 16)
                lanes = jnp.zeros((16, 128), jnp.float32)
                for c in range(0, depth, deep):
                    part = held[i, at, c : c + deep].astype(jnp.float32)
                    lanes = lane_sum(part * part, lanes)
                    part = part * gains_ref[:, ds + c : ds + c + deep].astype(jnp.float32)
                    scaled[to, c : c + deep] = part.astype(jnp.bfloat16)
                square_ref[to, :] = lanes
                return 0

            lax.fori_loop(0, tok // 16, scale_rows, 0, unroll=4)
        value_copy.wait()
        product = jnp.dot(scaled[...], value_held[...], preferred_element_type=jnp.float32)
        ones = jnp.ones((8, 128), jnp.bfloat16)
        across = (((1,), (1,)), ((), ()))
        rest = square_ref[...]
        square = jnp.zeros((8, number * tok), jnp.float32)
        for _ in range(3):
            piece = rest.astype(jnp.bfloat16)
            rest = rest - piece.astype(jnp.float32)
            square += lax.dot_general(ones, piece, across, preferred_element_type=jnp.float32)
        square = square * (SQUARE_FACTOR / dt)
        first = square.astype(jnp.bfloat16).astype(jnp.float32)
        rest = (square - first) * 256.0
        second = rest.astype(jnp.bfloat16).astype(jnp.float32)
        third = (rest - second) * 256.0
        row = lax.broadcasted_iota(jnp.int32, (8, number * tok), 0)
        split = jnp.where(row == 0, first, jnp.where(row == 1, second, third))
        for i, out_ref in enumerate(out_refs):
            out_ref[:tok, :] = product[i * tok : (i + 1) * tok, :] * factor
            out_ref[tok:, :] = jnp.zeros((EXTRA_ROWS, kv), jnp.float32)
            out_ref[tok : tok + 8, :tok] = split[:, i * tok : (i + 1) * tok]
        out_copies.append(pltpu.make_async_copy(kept_ref, kept_out, sems.at[last + shared]))
        out_copies[-1].start()
        for copy in out_copies:
            copy.wait()

    feature_shapes = [((tok, wide), jnp.bfloat16)] * cores
    feature_shapes += [((cores * tok, wide), jnp.bfloat16)] * (chips - 1)
    results = call(
        kernel,
        places,
        [student, hidden, value, jnp.concatenate([student_gain, gain]).reshape(1, ds + depth)],
        3,
        feature_shapes + [((tok + EXTRA_ROWS, kv), jnp.float32)] * number,
        [pltpu.VMEM(shape, dtype) for shape, dtype in feature_shapes]
        + [
            pltpu.VMEM((tok, ds), jnp.bfloat16),
            pltpu.VMEM((number, tok, depth), jnp.bfloat16),
            pltpu.VMEM((depth, kv), jnp.bfloat16),
            pltpu.VMEM((number * tok, depth), jnp.bfloat16),
            pltpu.VMEM((number * tok, 128), jnp.float32),
            pltpu.VMEM((tok + EXTRA_ROWS, kv), jnp.float32),
            pltpu.SemaphoreType.DMA((pieces + number + 2 + shared,)),
        ],
        "prepare",
        [*range(shared), shared + number - 1],
    )
    return results[:cores], results[cores:shared], results[shared:]


def states_parts(columns, features, values, rows, factor, early):
    cores, chips = len(values), len(features)
    tok, wide = features[0][0].shape
    tok = tok * len(features[0]) // cores
    kv = values[0][0].shape[1]
    flat = [v for of_core in values for v in of_core]
    spots = [
        (h, n, b)
        for h, of_core in enumerate(values)
        for n, v in enumerate(of_core)
        for b in range(v.shape[0] // rows)
    ]
    each = len(values[0])
    per_core = len(spots) // cores
    arrays = [part for of_chip in features for part in of_chip]
    place, first = [], 0
    for of_chip in features:
        split = len(of_chip) == cores
        place.append([(first + h, 0) if split else (first, h * tok) for h in range(cores)])
        first += len(of_chip)
    alone = [first for first, of_chip in enumerate(features) if len(of_chip) < cores]
    if rows % 128:
        totals = []
        for j in range(chips):
            total = jnp.zeros((tok, kv), jnp.float32)
            for i, (h, n, b) in enumerate(spots):
                array, above = place[j][h]
                at = (above, columns[i % per_core] * rows)
                part = lax.dynamic_slice(arrays[array], at, (tok, rows))
                block = lax.slice_in_dim(values[h][n], b * rows, (b + 1) * rows)
                total += jnp.dot(part, block, preferred_element_type=jnp.float32)
            totals.append(total * factor)
        return totals, [features[j][-1][-tok:] for j in alone]


    def kernel(columns_ref, *refs):
        own_refs, rest, refs = refs[:early], refs[early : len(arrays)], refs[len(arrays) :]
        value_refs, refs = refs[: len(flat)], refs[len(flat) :]
        out_refs, own_held, (own_ref, sems) = refs[: -2 - early], refs[-2 - early : -2], refs[-2:]
        own_copies = []
        for n in range(early):
            own_copies.append(pltpu.make_async_copy(own_refs[n], own_held[n], sems.at[n]))
            own_copies[-1].start()
        feature_refs = [*own_held, *rest]
        copies = []
        for n, j in enumerate(alone):
            src = feature_refs[place[j][0][0]].at[pl.ds((cores - 1) * tok, tok)]
            copies.append(pltpu.make_async_copy(src, out_refs[chips + n], sems.at[early + 1 + n]))
            copies[-1].start()
        for j in range(chips):
            if j == 0:
                for copy in own_copies:
                    copy.wait()
            total = jnp.zeros((tok, kv), jnp.float32)
            for i, (h, n, b) in enumerate(spots):
                start = pl.multiple_of(columns_ref[i % per_core] * rows, rows)
                array, above = place[j][h]
                total += jnp.dot(
                    feature_refs[array][above : above + tok, pl.ds(start, rows)],
                    value_refs[h * each + n][b * rows : (b + 1) * rows, :],
                    preferred_element_type=jnp.float32,
                )
            out_refs[j][...] = total * factor
        for copy in copies:
            copy.wait()

    out = [((tok, kv), jnp.float32)] * chips + [((tok, wide), jnp.bfloat16)] * len(alone)
    scratch = [pltpu.VMEM(part.shape, part.dtype) for part in arrays[:early]]
    scratch += [pltpu.VMEM((tok, kv), jnp.float32)]
    scratch += [pltpu.SemaphoreType.DMA((early + 1 + len(alone),))]
    out_hbm = range(chips, len(out))
    results = call(
        kernel, columns, [*arrays, *flat], early, out, scratch, "states_parts", out_hbm
    )
    return results[:chips], results[chips:]


def turned(columns, blocks, rows):
    number = columns.shape[0]
    tok = blocks[0].shape[0]

    def kernel(columns_ref, first_ref, *refs):
        block_refs, (out_ref, first_held, sem) = refs[:-3], refs[-3:]
        copy = pltpu.make_async_copy(first_ref, first_held, sem.at[0])
        copy.start()
        for b, block_ref in [*enumerate(block_refs, 1), (0, first_held)]:
            if b == 0:
                copy.wait()
            for i in range(number):
                src = pl.ds(pl.multiple_of(columns_ref[i] * rows, rows), rows)
                out_ref[i * rows : (i + 1) * rows, b * tok : (b + 1) * tok] = block_ref[:tok, src].T

    out = [((number * rows, len(blocks) * tok), jnp.bfloat16)]
    scratch = [pltpu.VMEM(blocks[0].shape, blocks[0].dtype), pltpu.SemaphoreType.DMA((1,))]
    return call(kernel, columns, blocks, 1, out, scratch, "turned")[0]


def gradient_blocks(held, seen, number, blocks, dtype):
    rows, tok = held.shape[0] // number, seen[0].shape[0]
    kv = seen[0].shape[1]

    def kernel(_, held_ref, *refs):
        seen_refs, out_refs = refs[: len(seen)], refs[len(seen) :]
        for i, out_ref in zip(blocks, out_refs):
            total = jnp.zeros((rows, kv), jnp.float32)
            for b, seen_ref in enumerate(seen_refs):
                total += jnp.dot(
                    held_ref[i * rows : (i + 1) * rows, b * tok : (b + 1) * tok],
                    seen_ref[...],
                    preferred_element_type=jnp.float32,
                )
            out_ref[...] = total.astype(out_ref.dtype)

    out = [((rows, kv), dtype)] * len(blocks)
    return call(kernel, jnp.zeros(1), [held, *seen], 0, out, [], "gradient_blocks")


def solution(mesh):
    sizes = dict(mesh.shape)
    grp, dp, mp = sizes["grp"], sizes["dp"], sizes["mp"]
    cores = 2 if dp % 2 == 0 else 1
    chips = dp // cores

    def swap(value, axis, step):
        return lax.ppermute(value, axis, [(i, i ^ step) for i in range(sizes[axis])])

    def per_device(
        teacher_hidden,
        teacher_gain,
        teacher_value,
        student_hidden,
        student_gain,
        student_value,
        segment_ids,
    ):
        f32, bf16, f16 = jnp.float32, jnp.bfloat16, jnp.float16
        tok, ds = student_hidden.shape
        kv_part = student_value.shape[1]
        rows = student_value.shape[0]
        dt_part = teacher_hidden.shape[1]
        dt, kv = dt_part * mp, kv_part * grp
        member = lax.axis_index("mp")
        place = lax.axis_index("dp")
        chip, core = place // cores, place % cores

        pieces = {0: student_value}
        step = mp // 2
        while step:
            pieces[step] = swap(student_value, "mp", step)
            step //= 2

        teacher_factor = half_scale(dt * HIDDEN_MAX * GAIN_MAX * TEACHER_VALUE_MAX)
        order = [2, 3, 1] + [0] if mp == 4 else list(range(1, mp)) + [0]
        own, others, parts = prepare(
            jnp.stack([member ^ k for k in order] + [chip, core]),
            student_hidden,
            student_gain,
            teacher_hidden,
            teacher_gain,
            teacher_value,
            chips,
            cores,
            dt,
            teacher_factor,
        )
        others = [swap(part, "dp", cores * (j + 1)) for j, part in enumerate(others)]
        *parts, kept = parts
        parts = [part.astype(f16) for part in parts]
        parts, pieces = lax.optimization_barrier((parts, pieces))
        received = [swap(part, "mp", k) for k, part in zip(order, parts)]

        first = list(pieces)
        later = []
        step = mp // 4
        while step:
            for o in [o for o in pieces if o >= 2 * step and o % (2 * step) == 0]:
                if o ^ step not in pieces:
                    pieces[o ^ step] = swap(pieces[o], "mp", step)
                    later.append(o ^ step)
            step //= 2
        gathered = [jnp.concatenate([pieces[o] for o in first], axis=0)]
        gathered += [pieces[o] for o in later]
        gathered[-1], received[2] = lax.optimization_barrier((gathered[-1], received[2]))
        gathered = [gathered]
        if cores == 2:
            gathered.append([swap(v, "dp", 1) for v in gathered[0]])

        columns = jnp.stack([member ^ o for o in first + later])
        states_factor = half_scale(GAIN_MAX * ds * STUDENT_VALUE_MAX)
        returned, second = states_parts(
            columns, [[part] for part in others], gathered, rows, states_factor, 0
        )
        (states,), _ = states_parts(columns, [own], gathered, rows, states_factor, len(own))
        if cores == 1:
            second = others
        returned = payload = [part.astype(f16) for part in returned]
        returned = [swap(part, "dp", cores * (j + 1)) for j, part in enumerate(returned)]

        held = [own[0], *others]
        if cores == 2:
            held += [swap(part, "dp", 1) for part in [own[1], *second]]
        line = mp == 4
        if line:
            inner = (member == 1) | (member == 2)
            turn_order = [(1, 3), (3, 2), (2, 1), (0, 0)]
            turn_order = [member ^ jnp.where(inner, i, o) for i, o in turn_order]
        else:
            turn_order = [member ^ k for k in order]
        turn_order = jnp.stack(turn_order)
        if rows % 128 == 0:
            held = turned(turn_order, held, rows)

        summed = kept
        for part in received:
            summed = summed + part.astype(f32)
        pieces = summed[tok : tok + 3, :tok]
        squares = pieces[0] + (pieces[1] + pieces[2] * (1.0 / 256.0)) * (1.0 / 256.0)
        teacher_scale = lax.rsqrt(squares * (1.0 / SQUARE_FACTOR) + norm_eps)
        projected = summed[:tok] * (1.0 / teacher_factor)
        target = projected * teacher_scale[:, None]
        power_half = jnp.sum(target * target, axis=1)
        power_half, payload = lax.optimization_barrier((power_half, payload))
        power = power_half
        for k in range(1, grp):
            power = power + swap(power_half, "grp", k)
        target_power = power / kv + power_eps

        for part in returned:
            states = states + part.astype(f32)
        states = states * (1.0 / states_factor)

        matches = segment_ids[:, :, None] == jnp.arange(NSEG, dtype=jnp.int32)[None, None, :]
        counts = jnp.sum(matches.astype(jnp.int32), axis=1)
        lengths = jnp.sum(jnp.where(matches, counts[:, None, :], 0), axis=2).reshape(-1)
        doc_length = lax.dynamic_slice_in_dim(lengths, member * tok, tok, 0).astype(f32)
        weighted = ((states - target) / (doc_length * target_power)[:, None]).astype(bf16)

        seen = [swap(weighted, "dp", cores * j) for j in range(1, chips)]
        held, seen = lax.optimization_barrier((held, seen))
        seen = [weighted] + seen
        if cores == 2:
            seen += [swap(part, "dp", 1) for part in seen]
        rounded = 2 if line else mp - 1
        if rows % 128:
            held = jnp.concatenate([part[:tok] for part in held], axis=0)
            seen = jnp.concatenate(seen, axis=0)
            parts = [
                lax.dot_general(
                    lax.dynamic_slice_in_dim(held, turn_order[i] * rows, rows, 1),
                    seen,
                    (((0,), (0,)), ((), ())),
                    preferred_element_type=f32,
                )
                for i in range(mp)
            ]
            parts = [p.astype(bf16) for p in parts[:rounded]] + parts[rounded:]
        else:
            parts = [
                *gradient_blocks(held, seen, mp, range(rounded), bf16),
                *gradient_blocks(held, seen, mp, range(rounded, mp), f32),
            ]
        if line:
            near = swap(parts[0], "mp", 1).astype(f32)
            past = lax.ppermute(parts[1], "mp", [(0, 2), (3, 1)])
            across = lax.ppermute(parts[1], "mp", [(1, 2), (2, 1)])
            last = (parts[2] + jnp.where(inner, near, 0.0)).astype(bf16)
            last = lax.ppermute(last, "mp", [(1, 3), (2, 0), (0, 1), (3, 2)])
            total = parts[3] + jnp.where(inner, 0.0, near)
            total = total + across.astype(f32) + past.astype(f32) + last.astype(f32)
        else:
            total = parts[-1]
            for i in range(mp - 1):
                total = total + swap(parts[i], "mp", order[i]).astype(f32)
        return total

    return jax.shard_map(
        per_device,
        mesh=mesh,
        in_specs=(
            P("dp", "mp"),
            P("mp"),
            P("mp", "grp"),
            P(("dp", "mp"), None),
            P(),
            P(("dp", "mp"), "grp"),
            P("dp", None),
        ),
        out_specs=P(("dp", "mp"), "grp"),
        check_vma=False,
    )
```
